32 devices in a mesh: pi: 4 (over x, core), pj: 8 (over z, y).
Axes of the slice: x: 2, y: 2, z: 4, core: 2. Of those that a mesh axis runs over, the one named last changes fastest.
Arguments:
- amplitudes: bfloat16 [8, 48, 8, 4096], P('pi', 'pj'), may hold values from -6 to 6
- coulomb: bfloat16 [48, 48, 8, 4096], P('pi', 'pj'), may hold values from -0.046875 to 0.046875
- exchange: bfloat16 [48, 48, 8, 4096], P('pi', 'pj'), may hold values from -0.046875 to 0.046875
- occ_irrep: int32 [48], replicated, may hold values from 0 to 7
Outputs:
- residual: bfloat16 [8, 48, 8, 4096], P('pi', 'pj')
The draws below stay inside these ranges and needn't reach their ends.
Inputs may be any that keep to these rules, and one draw needn't show every extreme that they name: `occ_irrep`: the virtual orbitals hold 64 of each of the 8 irreps and are stored irrep by irrep.
All inputs are finite; a program needn't handle non-finite values.
Results may differ from the reference program's by a relative error of at most 0.0058.
Values may be sent and summed in bfloat16 or wider, within the bound.
A program may use at most 384 MiB of HBM per device.

```python
import jax
import jax.numpy as jnp
from jax import lax

NO = 48
NVI = 64
NI = 8


def plant(drawn, rng, least, high):
    index_at = [jax.random.randint(jax.random.fold_in(rng, axis), (), 0, length) for axis, length in enumerate(drawn.shape)]
    main_axis = drawn.shape.index(max(drawn.shape))
    neighbour = index_at[:main_axis] + [(index_at[main_axis] + 1) % drawn.shape[main_axis]] + index_at[main_axis + 1:]
    return drawn.at[tuple(index_at)].set(least).at[tuple(neighbour)].set(high)


def level_of(own_key, dims, cuts, least, top_value):
    def one(dim, shards_of):
        draws = jax.random.uniform(jax.random.fold_in(jax.random.fold_in(own_key, 6), dim), (shards_of,), jnp.float32, least / len(cuts), top_value / len(cuts))
        return jnp.repeat(jnp.exp(draws), dims[dim] // shards_of).reshape((-1,) + (1,) * (len(dims) - dim - 1))

    level = one(*cuts[0])
    for cut in cuts[1:]:
        level = level * one(*cut)
    return level


def normal_values(own_key, extent, spread, limit, pieces=(), held_as=jnp.bfloat16):
    gain = level_of(own_key, extent, pieces, -0.22, 0.18) if pieces else 1.0
    drawn = jax.random.normal(own_key, extent, jnp.float32) * spread * gain
    return jnp.minimum(jnp.maximum(drawn, -limit), limit).astype(held_as)


def setup_inputs(seed: int = 0) -> dict:
    keys = jax.random.split(jax.random.key(seed), 5)
    amplitudes = normal_values(keys[0], (NI, NO, 8, NVI * NVI), 1.0, 6.0, ((0, 4), (1, 8)))
    coulomb = normal_values(keys[1], (NO, NO, 8, NVI * NVI), (5 * NO * NVI) ** -0.5, 0.046875, ((0, 4), (1, 8)))
    exchange = normal_values(keys[2], (NO, NO, 8, NVI * NVI), (5 * NO * NVI) ** -0.5, 0.046875, ((0, 4), (1, 8)))
    occ_irrep = plant(jax.random.randint(keys[3], (NO,), 0, 8), jax.random.fold_in(keys[3], 1), 0, 7).astype(jnp.int32)
    return dict(amplitudes=amplitudes, coulomb=coulomb, exchange=exchange, occ_irrep=occ_irrep)


def reference(amplitudes, coulomb, exchange, occ_irrep):
    blocks = jnp.arange(8, dtype=jnp.int32)
    orbital = jnp.arange(NO, dtype=jnp.int32)
    first = jnp.arange(NI, dtype=jnp.int32)
    amp_blocks = amplitudes.reshape(NI, NO, 8, NVI, NVI)
    pair = jnp.bitwise_xor(occ_irrep[:, None], occ_irrep[None, :]).astype(jnp.int32)
    select_kj = jnp.bitwise_xor(blocks[None, None, :], pair[:, :, None]).astype(jnp.int32)
    select_ik = select_kj[:NI]
    swapped = amp_blocks[first[:, None, None], orbital[None, :, None], select_ik]
    doubled = (2.0 * amp_blocks.astype(jnp.float32) - jnp.swapaxes(swapped, 3, 4).astype(jnp.float32)).astype(jnp.bfloat16)
    ladder = (2.0 * coulomb.astype(jnp.float32) - exchange.astype(jnp.float32)).astype(jnp.bfloat16)
    ladder = ladder.reshape(NO, NO, 8, NVI, NVI)
    cross_ladder = ladder[orbital[:, None, None], orbital[None, :, None], select_kj]

    def one_row(packed):
        row_doubled, row_amp, row_select = packed
        direct_ladder = ladder[orbital[:, None, None], orbital[None, :, None], row_select[:, None, :]]
        direct = jnp.einsum("khac,kjhcb->jhab", row_doubled.astype(jnp.float32), direct_ladder.astype(jnp.float32))
        cross_amp = row_amp[orbital[:, None, None], select_kj]
        crossed = jnp.einsum("kjhca,kjhcb->jhab", cross_ladder.astype(jnp.float32), cross_amp.astype(jnp.float32))
        return (direct - crossed).astype(jnp.bfloat16)

    result = lax.map(one_row, (doubled, amp_blocks, select_ik))
    return result.reshape(NI, NO, 8, NVI * NVI)
```

```python
import functools

import jax
import jax.numpy as jnp
from jax import lax
from jax.experimental import pallas as pl
from jax.experimental.pallas import tpu as pltpu
from jax.sharding import PartitionSpec as P

V = 64
H = 8
T = V // 2
MESH = pl.DeviceIdType.MESH
F32 = jnp.float32
BF16 = jnp.bfloat16
NT = (((1,), (1,)), ((), ()))


def even_odd_pair():
    row = lax.broadcasted_iota(jnp.int32, (2 * V, 2 * V), 0)
    col = lax.broadcasted_iota(jnp.int32, (2 * V, 2 * V), 1)
    inside = row % V
    source = (row // V) * V + 2 * (inside % T) + inside // T
    return (col == source).astype(F32).astype(BF16)


def low_half(shape):
    return lax.broadcasted_iota(jnp.int32, shape, len(shape) - 1) < V


def pair_up(first, second):
    low = low_half(first.shape)
    axis = first.ndim - 1
    return (
        jnp.where(low, first, pltpu.roll(second, V, axis)),
        jnp.where(low, pltpu.roll(first, V, axis), second),
    )


def split_rows(row):
    return row.reshape(H, T, 2 * V)


def stack(first, second):
    even, odd = pair_up(first, second)
    return jnp.concatenate([even, odd], axis=1).astype(BF16)


def ladder_part(kp, nk, nj, c_ref, x_ref, ls_ref, lt_ref):
    perm = even_odd_pair()

    def ladder(k, j):
        return split_rows(2.0 * c_ref[k, j].astype(F32) - x_ref[k, j].astype(F32))

    for jp in range((nj + 1) // 2):
        tiles = []
        for kk in range(2):
            k = 2 * kp + kk
            if nk % 2 and kk == 1:
                safe = jnp.minimum(k, nk - 1)
                keep = (k < nk).astype(F32)
            else:
                safe, keep = k, None
            first = ladder(safe, 2 * jp)
            second = ladder(safe, 2 * jp + 1) if 2 * jp + 1 < nj else jnp.zeros_like(first)
            tile = stack(first, second)
            if keep is not None:
                tile = (tile.astype(F32) * keep).astype(BF16)
            ls_ref[k, :, :, 2 * V * jp:2 * V * (jp + 1)] = tile
            tiles.append(tile)
        for h in range(H):
            both = jnp.concatenate([tiles[0][h], tiles[1][h]], axis=0)
            turned = lax.dot_general(perm, both, NT, preferred_element_type=F32).astype(BF16)
            lt_ref[2 * jp, h, kp] = turned[:V]
            lt_ref[2 * jp + 1, h, kp] = turned[V:]


def gather_kernel(npi, fold, rows, nk, nj, amp_ref, c_hbm, x_hbm, all_ref, ls_ref, lt_ref,
                  col, c_ref, x_ref, c_sem, x_sem, own_sem, local_sem, col_recv, up_send, down_send,
                  x_recv, x_send, y_recv, y_send):
    p = lax.axis_index("pi")
    q = lax.axis_index("pj")
    z = q // fold
    y = q % fold
    barrier = pltpu.get_barrier_semaphore()
    up = (p, q + fold)
    down = (p, q - fold)

    @pl.when(z + 1 < npi)
    def _():
        pl.semaphore_signal(barrier, inc=1, device_id=up, device_id_type=MESH)

    @pl.when(z > 0)
    def _():
        pl.semaphore_signal(barrier, inc=1, device_id=down, device_id_type=MESH)

    for step in range(1, npi):
        pl.semaphore_signal(barrier, inc=1, device_id=((p + step) % npi, q), device_id_type=MESH)
    for step in range(1, fold):
        pl.semaphore_signal(barrier, inc=1, device_id=(p, z * fold + (y + step) % fold), device_id_type=MESH)

    load_c = pltpu.make_async_copy(c_hbm, c_ref, c_sem)
    load_x = pltpu.make_async_copy(x_hbm, x_ref, x_sem)
    own = pltpu.make_async_copy(amp_ref, col.at[z], own_sem)
    own.start()
    load_c.start()
    load_x.start()

    at_end = (z == 0) | (z == npi - 1)

    @pl.when(at_end)
    def _():
        pl.semaphore_wait(barrier, npi + fold - 1)

    @pl.when(jnp.logical_not(at_end))
    def _():
        pl.semaphore_wait(barrier, npi + fold)

    own.wait()

    def send_up(piece, ch):
        return pltpu.make_async_remote_copy(
            src_ref=col.at[piece, ch], dst_ref=col.at[piece, ch], send_sem=up_send.at[piece, ch],
            recv_sem=col_recv.at[piece, ch], device_id=up, device_id_type=MESH)

    def send_down(piece, ch):
        return pltpu.make_async_remote_copy(
            src_ref=col.at[piece, ch], dst_ref=col.at[piece, ch], send_sem=down_send.at[piece, ch],
            recv_sem=col_recv.at[piece, ch], device_id=down, device_id_type=MESH)

    def send_x(piece, ch):
        return pltpu.make_async_remote_copy(
            src_ref=col.at[piece, ch], dst_ref=all_ref.at[p, y, ch], send_sem=x_send.at[piece, ch],
            recv_sem=x_recv.at[p, ch], device_id=(piece, q), device_id_type=MESH)

    def keep(ch):
        return pltpu.make_async_copy(col.at[p, ch], all_ref.at[p, y, ch], local_sem.at[ch])

    def send_y(source, ch, step):
        return pltpu.make_async_remote_copy(
            src_ref=all_ref.at[source, y, ch], dst_ref=all_ref.at[source, y, ch],
            send_sem=y_send.at[source, step, ch], recv_sem=y_recv.at[source, y, ch],
            device_id=(p, z * fold + (y + step) % fold), device_id_type=MESH)

    def place(piece, ch):
        @pl.when(piece != p)
        def _():
            send_x(piece, ch).start()

        @pl.when(piece == p)
        def _():
            keep(ch).start()

    def forward_y(when):
        if fold > 1:
            @pl.when(when)
            def _():
                for ch in range(rows):
                    for shift in range(npi):
                        source = (p + shift) % npi
                        if shift == 0:
                            keep(ch).wait()
                        else:
                            send_x_from(source, ch).wait_recv()
                        for step in range(1, fold):
                            send_y(source, ch, step).start()

    def send_x_from(source, ch):
        return pltpu.make_async_remote_copy(
            src_ref=col.at[0, ch], dst_ref=all_ref.at[source, y, ch], send_sem=x_send.at[0, ch],
            recv_sem=x_recv.at[source, ch], device_id=(source, q), device_id_type=MESH)

    for ch in range(rows):
        @pl.when(z + 1 < npi)
        def _():
            send_up(z, ch).start()

        @pl.when(z > 0)
        def _():
            send_down(z, ch).start()

        place(z, ch)

    load_c.wait()
    load_x.wait()

    @pl.loop(0, (nk + 1) // 2)
    def _(kp):
        ladder_part(kp, nk, nj, c_ref, x_ref, ls_ref, lt_ref)

    away = jnp.where(z > p, z - p, p - z)
    for far in range(1, npi):
        for ch in range(rows):
            below = z - far
            above = z + far

            @pl.when(below >= 0)
            def _():
                send_up(below, ch).wait_recv()

                @pl.when(z + 1 < npi)
                def _():
                    send_up(below, ch).start()

                place(below, ch)

            @pl.when(above < npi)
            def _():
                send_down(above, ch).wait_recv()

                @pl.when(z > 0)
                def _():
                    send_down(above, ch).start()

                place(above, ch)
        forward_y(away == far - 1)
    forward_y(away == npi - 1)

    for ch in range(rows):
        if fold == 1:
            keep(ch).wait()
            for shift in range(1, npi):
                send_x_from((p + shift) % npi, ch).wait_recv()
        for source in range(npi):
            for step in range(1, fold):
                other = (y + step) % fold
                pltpu.make_async_remote_copy(
                    src_ref=all_ref.at[source, other, ch], dst_ref=all_ref.at[source, other, ch],
                    send_sem=y_send.at[source, step, ch], recv_sem=y_recv.at[source, other, ch],
                    device_id=(p, z * fold + other), device_id_type=MESH).wait_recv()
                send_y(source, ch, step).wait_send()
        for piece in range(npi):
            @pl.when((piece <= z) & (z + 1 < npi))
            def _():
                send_up(piece, ch).wait_send()

            @pl.when((piece >= z) & (z > 0))
            def _():
                send_down(piece, ch).wait_send()

            @pl.when(piece != p)
            def _():
                send_x(piece, ch).wait_send()


def contract_kernel(npi, first_i, fold, rows, nka, nj, label_ref, all_ref, ls_ref, lt_ref, out_ref,
                    as_ref, qs_ref, qt_ref, direct, crossed):
    p = lax.axis_index("pi")
    q = lax.axis_index("pj")
    ni = npi * rows
    nk = fold * nka
    nkp = (nk + 1) // 2
    njp = (nj + 1) // 2
    first_k = p * nk
    first_j = q * nj
    perm = even_odd_pair()
    low = low_half((V, 2 * V))

    def k_label(k):
        return label_ref[first_k + min(k, nk - 1)]

    @pl.loop(0, ni // 2)
    def _(ip):
        for kp in range(nkp):
            def block(ii, kk):
                i = 2 * ip + ii
                k = 2 * kp + kk
                if k >= nk:
                    return jnp.zeros((H, T, 2 * V), F32)
                return split_rows(all_ref[i // rows, k // nka, i % rows, k % nka].astype(F32))

            b00, b01, b10, b11 = block(0, 0), block(0, 1), block(1, 0), block(1, 1)
            side0 = stack(b00, b10)
            side1 = stack(b01, b11)
            as_ref[ip, :, 2 * kp] = side0
            as_ref[ip, :, 2 * kp + 1] = side1
            along0 = stack(b00, b01)
            along1 = stack(b10, b11)
            for h in range(H):
                both = jnp.concatenate([side0[h], side1[h]], axis=0)
                turned = lax.dot_general(perm, both, NT, preferred_element_type=F32).astype(BF16)
                qt_ref[2 * ip, h, kp] = turned[:V]
                qt_ref[2 * ip + 1, h, kp] = turned[V:]
                both = jnp.concatenate([along0[h], along1[h]], axis=0)
                moved = lax.dot_general(both, perm, NT, preferred_element_type=F32).astype(BF16)
                qs_ref[2 * ip, h, kp] = moved[:V]
                qs_ref[2 * ip + 1, h, kp] = moved[V:]

    @pl.loop(0, ni)
    def _(i):
        label = label_ref[first_i + i]
        pairs = [label ^ k_label(k) for k in range(2 * nkp)]

        @pl.loop(0, H)
        def _(h):
            left, right = [], []
            for kp in range(nkp):
                g0 = h ^ pairs[2 * kp]
                g1 = h ^ pairs[2 * kp + 1]
                turned = jnp.where(low, qt_ref[i, g0, kp].astype(F32), qt_ref[i, g1, kp].astype(F32))
                left.append((2.0 * qs_ref[i, h, kp].astype(F32) - turned).astype(BF16))
                right += [ls_ref[2 * kp, g0], ls_ref[2 * kp + 1, g1]]
            direct[i, h] = jnp.dot(
                jnp.concatenate(left, axis=1), jnp.concatenate(right, axis=0), preferred_element_type=F32)

    @pl.loop(0, nj)
    def _(j):
        label = label_ref[first_j + j]
        pairs = [label ^ k_label(k) for k in range(2 * nkp)]

        @pl.loop(0, H)
        def _(h):
            left = []
            for kp in range(nkp):
                g0 = h ^ pairs[2 * kp]
                g1 = h ^ pairs[2 * kp + 1]
                left.append(jnp.where(low, lt_ref[j, g0, kp].astype(F32), lt_ref[j, g1, kp].astype(F32)).astype(BF16))
            left = jnp.concatenate(left, axis=1)

            for ip in range(0, ni // 2, 2):
                right = jnp.concatenate(
                    [jnp.concatenate([as_ref[ip, h ^ pairs[k], k], as_ref[ip + 1, h ^ pairs[k], k]], axis=1)
                     for k in range(2 * nkp)], axis=0)
                both = jnp.dot(left, right, preferred_element_type=F32)
                crossed[j, ip, h] = both[:, :2 * V]
                crossed[j, ip + 1, h] = both[:, 2 * V:]

    @pl.loop(0, ni // 2)
    def _(ip):
        for jp in range(njp):
            lanes = slice(2 * V * jp, 2 * V * (jp + 1))

            def halves(tile):
                return pair_up(tile[:, :T], tile[:, T:])

            d = [halves(direct[2 * ip + ii, :, :, lanes]) for ii in range(2)]
            for jj in range(2):
                j = 2 * jp + jj
                if j >= nj:
                    continue
                c = halves(crossed[j, ip])
                for ii in range(2):
                    i = 2 * ip + ii
                    result = (d[ii][jj] - c[ii]).reshape(H, V * V).astype(BF16)
                    out_ref[i // rows, i % rows, j] = result


def scatter_kernel(npi, part_ref, out_ref, near, sums, far, near_send, near_recv, far_send, far_recv):
    p = lax.axis_index("pi")
    q = lax.axis_index("pj")
    core = p % 2
    chip = p // 2
    chips = npi // 2
    mate = chip * 2 + 1 - core
    barrier = pltpu.get_barrier_semaphore()
    pl.semaphore_signal(barrier, inc=1, device_id=(mate, q), device_id_type=MESH)
    for step in range(1, chips):
        pl.semaphore_signal(barrier, inc=1, device_id=((chip + step) % chips * 2 + core, q), device_id_type=MESH)
    pl.semaphore_wait(barrier, chips)

    def to_mate(step):
        target = (chip + step) % chips
        return pltpu.make_async_remote_copy(
            src_ref=part_ref.at[target * 2 + 1 - core], dst_ref=near.at[step], send_sem=near_send.at[step],
            recv_sem=near_recv.at[step], device_id=(mate, q), device_id_type=MESH)

    def to_chip(step):
        return pltpu.make_async_remote_copy(
            src_ref=sums.at[step], dst_ref=far.at[step], send_sem=far_send.at[step],
            recv_sem=far_recv.at[step], device_id=((chip + step) % chips * 2 + core, q), device_id_type=MESH)

    order = [*range(1, chips), 0]
    for step in order:
        to_mate(step).start()
    for step in order:
        to_mate(step).wait_recv()
        if step:
            @pl.loop(0, out_ref.shape[0])
            def _(i):
                sums[step, i] = (part_ref[(chip + step) % chips * 2 + core, i].astype(F32)
                                 + near[step, i].astype(F32)).astype(BF16)
            to_chip(step).start()
    for step in range(1, chips):
        to_chip(step).wait_recv()

    @pl.loop(0, out_ref.shape[0])
    def _(i):
        total = part_ref[p, i].astype(F32) + near[0, i].astype(F32)
        for step in range(1, chips):
            total = total + far[step, i].astype(F32)
        out_ref[i] = total.astype(BF16)

    for step in order:
        to_mate(step).wait_send()
        if step:
            to_chip(step).wait_send()


def on_device(npi, fold, amplitudes, coulomb, exchange, occ_irrep):
    rows, nka = amplitudes.shape[:2]
    nk, nj = coulomb.shape[:2]
    nkp, njp = (nk + 1) // 2, (nj + 1) // 2
    vmem = pl.BlockSpec(memory_space=pltpu.VMEM)
    hbm = pl.BlockSpec(memory_space=pl.ANY)
    smem = pl.BlockSpec(memory_space=pltpu.SMEM)
    dma = pltpu.SemaphoreType.DMA
    limit = 60 * 2**20
    gathered, ls, lt = pl.pallas_call(
        functools.partial(gather_kernel, npi, fold, rows, nk, nj),
        out_shape=(
            jax.ShapeDtypeStruct((npi, fold) + amplitudes.shape, BF16),
            jax.ShapeDtypeStruct((2 * nkp, H, V, 2 * V * njp), BF16),
            jax.ShapeDtypeStruct((2 * njp, H, nkp, V, 2 * V), BF16),
        ),
        in_specs=[hbm, hbm, hbm],
        out_specs=(vmem, vmem, vmem),
        scratch_shapes=[
            pltpu.VMEM((npi,) + amplitudes.shape, BF16),
            pltpu.VMEM(coulomb.shape, BF16),
            pltpu.VMEM(coulomb.shape, BF16),
            dma(()), dma(()), dma(()), dma((rows,)),
            dma((npi, rows)), dma((npi, rows)), dma((npi, rows)),
            dma((npi, rows)), dma((npi, rows)),
            dma((npi, fold, rows)), dma((npi, fold, rows)),
        ],
        compiler_params=pltpu.CompilerParams(collective_id=0, has_side_effects=True, vmem_limit_bytes=limit),
    )(amplitudes, coulomb, exchange)
    parts = []
    span = min(npi, 8 // rows)
    ni = span * rows
    for first in range(0, npi, span):
        parts.append(pl.pallas_call(
            functools.partial(contract_kernel, span, first * rows, fold, rows, nka, nj),
            out_shape=jax.ShapeDtypeStruct((span, rows, nj) + amplitudes.shape[2:], BF16),
            in_specs=[smem, vmem, vmem, vmem],
            out_specs=vmem,
            scratch_shapes=[
                pltpu.VMEM((ni // 2, H, 2 * nkp, V, 2 * V), BF16),
                pltpu.VMEM((ni, H, nkp, V, 2 * V), BF16),
                pltpu.VMEM((ni, H, nkp, V, 2 * V), BF16),
                pltpu.VMEM((ni, H, V, 2 * V * njp), F32),
                pltpu.VMEM((nj, ni // 2, H, V, 2 * V), F32),
            ],
            compiler_params=pltpu.CompilerParams(vmem_limit_bytes=limit),
        )(occ_irrep, gathered[first:first + span], ls, lt))
    parts = parts[0] if len(parts) == 1 else jnp.concatenate(parts)
    piece = (rows, nj) + amplitudes.shape[2:]
    chips = npi // 2
    return pl.pallas_call(
        functools.partial(scatter_kernel, npi),
        out_shape=jax.ShapeDtypeStruct(piece, BF16),
        in_specs=[vmem],
        out_specs=vmem,
        scratch_shapes=[
            pltpu.VMEM((chips,) + piece, BF16),
            pltpu.VMEM((chips,) + piece, BF16),
            pltpu.VMEM((chips,) + piece, BF16),
            dma((chips,)), dma((chips,)), dma((chips,)), dma((chips,)),
        ],
        compiler_params=pltpu.CompilerParams(collective_id=1, has_side_effects=True, vmem_limit_bytes=limit),
    )(parts)


def solution(mesh):
    npi, npj = mesh.shape["pi"], mesh.shape["pj"]
    placed = (P("pi", "pj", None, None), P("pi", "pj", None, None), P("pi", "pj", None, None), P())
    return jax.shard_map(
        functools.partial(on_device, npi, npj // npi), mesh=mesh, in_specs=placed,
        out_specs=P("pi", "pj", None, None), check_vma=False
    )
```

```python
import functools

import jax
import jax.numpy as jnp
from jax import lax
from jax.experimental import pallas as pl
from jax.experimental.pallas import tpu as pltpu
from jax.sharding import PartitionSpec as P

V = 64
H = 8
T = V // 2
MESH = pl.DeviceIdType.MESH
F32 = jnp.float32
BF16 = jnp.bfloat16
NT = (((1,), (1,)), ((), ()))


def even_odd_pair():
    row = lax.broadcasted_iota(jnp.int32, (2 * V, 2 * V), 0)
    col = lax.broadcasted_iota(jnp.int32, (2 * V, 2 * V), 1)
    inside = row % V
    source = (row // V) * V + 2 * (inside % T) + inside // T
    return (col == source).astype(F32).astype(BF16)


def low_half(shape):
    return lax.broadcasted_iota(jnp.int32, shape, len(shape) - 1) < V


def pair_up(first, second):
    low = low_half(first.shape)
    axis = first.ndim - 1
    return (
        jnp.where(low, first, pltpu.roll(second, V, axis)),
        jnp.where(low, pltpu.roll(first, V, axis), second),
    )


def split_rows(row):
    return row.reshape(H, T, 2 * V)


def stack(first, second):
    even, odd = pair_up(first, second)
    return jnp.concatenate([even, odd], axis=1).astype(BF16)


def ladder_part(kp, nk, nj, c_ref, x_ref, ls_ref, lt_ref):
    perm = even_odd_pair()

    def ladder(k, j):
        return split_rows(2.0 * c_ref[k, j].astype(F32) - x_ref[k, j].astype(F32))

    for jp in range((nj + 1) // 2):
        tiles = []
        for kk in range(2):
            k = 2 * kp + kk
            if k >= nk:
                tile = jnp.zeros((H, V, 2 * V), BF16)
                ls_ref[k, :, :, 2 * V * jp:2 * V * (jp + 1)] = tile
                tiles.append(tile)
                continue
            first = ladder(k, 2 * jp)
            second = ladder(k, 2 * jp + 1) if 2 * jp + 1 < nj else jnp.zeros_like(first)
            tile = stack(first, second)
            ls_ref[k, :, :, 2 * V * jp:2 * V * (jp + 1)] = tile
            tiles.append(tile)
        for h in range(H):
            both = jnp.concatenate([tiles[0][h], tiles[1][h]], axis=0)
            turned = lax.dot_general(perm, both, NT, preferred_element_type=F32).astype(BF16)
            lt_ref[2 * jp, h, kp] = turned[:V]
            lt_ref[2 * jp + 1, h, kp] = turned[V:]


def gather_kernel(npi, fold, chunks, nk, nj, amp_ref, c_hbm, x_hbm, all_ref, ls_ref, lt_ref,
                  col, c_ref, x_ref, c_sem, x_sem, own_sem, local_sem, col_recv, up_send, down_send,
                  x_recv, x_send, y_recv, y_send):
    p = lax.axis_index("pi")
    q = lax.axis_index("pj")
    z = q // fold
    y = q % fold
    barrier = pltpu.get_barrier_semaphore()
    up = (p, q + fold)
    down = (p, q - fold)

    @pl.when(z + 1 < npi)
    def _():
        pl.semaphore_signal(barrier, inc=1, device_id=up, device_id_type=MESH)

    @pl.when(z > 0)
    def _():
        pl.semaphore_signal(barrier, inc=1, device_id=down, device_id_type=MESH)

    for step in range(1, npi):
        pl.semaphore_signal(barrier, inc=1, device_id=((p + step) % npi, q), device_id_type=MESH)
    for step in range(1, fold):
        pl.semaphore_signal(barrier, inc=1, device_id=(p, z * fold + (y + step) % fold), device_id_type=MESH)

    load_c = pltpu.make_async_copy(c_hbm, c_ref, c_sem)
    load_x = pltpu.make_async_copy(x_hbm, x_ref, x_sem)
    own = pltpu.make_async_copy(amp_ref, col.at[z], own_sem)
    own.start()
    load_c.start()
    load_x.start()

    at_end = (z == 0) | (z == npi - 1)

    @pl.when(at_end)
    def _():
        pl.semaphore_wait(barrier, npi + fold - 1)

    @pl.when(jnp.logical_not(at_end))
    def _():
        pl.semaphore_wait(barrier, npi + fold)

    own.wait()

    def send_up(piece, ch):
        return pltpu.make_async_remote_copy(
            src_ref=col.at[piece, ch], dst_ref=col.at[piece, ch], send_sem=up_send.at[piece, ch],
            recv_sem=col_recv.at[piece, ch], device_id=up, device_id_type=MESH)

    def send_down(piece, ch):
        return pltpu.make_async_remote_copy(
            src_ref=col.at[piece, ch], dst_ref=col.at[piece, ch], send_sem=down_send.at[piece, ch],
            recv_sem=col_recv.at[piece, ch], device_id=down, device_id_type=MESH)

    def send_x(piece, ch):
        return pltpu.make_async_remote_copy(
            src_ref=col.at[piece, ch], dst_ref=all_ref.at[p, y, ch], send_sem=x_send.at[piece, ch],
            recv_sem=x_recv.at[p, ch], device_id=(piece, q), device_id_type=MESH)

    def keep(ch):
        return pltpu.make_async_copy(col.at[p, ch], all_ref.at[p, y, ch], local_sem.at[ch])

    def send_y(source, ch, step):
        return pltpu.make_async_remote_copy(
            src_ref=all_ref.at[source, y, ch], dst_ref=all_ref.at[source, y, ch],
            send_sem=y_send.at[source, step, ch], recv_sem=y_recv.at[source, y, ch],
            device_id=(p, z * fold + (y + step) % fold), device_id_type=MESH)

    def send_own_y(ch, step):
        return pltpu.make_async_remote_copy(
            src_ref=col.at[p, ch], dst_ref=all_ref.at[p, y, ch],
            send_sem=y_send.at[p, step, ch], recv_sem=y_recv.at[p, y, ch],
            device_id=(p, z * fold + (y + step) % fold), device_id_type=MESH)

    def place(piece, ch):
        @pl.when(piece != p)
        def _():
            send_x(piece, ch).start()

        @pl.when(piece == p)
        def _():
            keep(ch).start()
            for step in range(1, fold):
                send_own_y(ch, step).start()

    away = jnp.where(z > p, z - p, p - z)
    lag = 2

    def forward_y(event):
        if fold > 1 and 0 <= event < npi * chunks:
            ch = event % chunks

            @pl.when(away == event // chunks)
            def _():
                for shift in range(1, npi):
                    source = (p + shift) % npi
                    send_x_from(source, ch).wait_recv()
                    for step in range(1, fold):
                        send_y(source, ch, step).start()

    def send_x_from(source, ch):
        return pltpu.make_async_remote_copy(
            src_ref=col.at[0, ch], dst_ref=all_ref.at[source, y, ch], send_sem=x_send.at[0, ch],
            recv_sem=x_recv.at[source, ch], device_id=(source, q), device_id_type=MESH)

    for ch in range(chunks):
        @pl.when(z + 1 < npi)
        def _():
            send_up(z, ch).start()

        @pl.when(z > 0)
        def _():
            send_down(z, ch).start()

        place(z, ch)

    load_c.wait()
    load_x.wait()
    parts = list(range((nk + 1) // 2))

    def some_ladder():
        if parts:
            ladder_part(parts.pop(0), nk, nj, c_ref, x_ref, ls_ref, lt_ref)

    some_ladder()
    for event in range(chunks, npi * chunks):
        far, ch = event // chunks, event % chunks
        below = z - far
        above = z + far

        @pl.when(below >= 0)
        def _():
            send_up(below, ch).wait_recv()

            @pl.when(z + 1 < npi)
            def _():
                send_up(below, ch).start()

            place(below, ch)

        @pl.when(above < npi)
        def _():
            send_down(above, ch).wait_recv()

            @pl.when(z > 0)
            def _():
                send_down(above, ch).start()

            place(above, ch)

        if event == chunks:
            for early in range(chunks - lag):
                forward_y(early)
        forward_y(event - lag)
        some_ladder()
    while parts:
        some_ladder()
    for late in range(npi * chunks - lag, npi * chunks):
        forward_y(late)

    for ch in range(chunks):
        keep(ch).wait()
        if fold == 1:
            for shift in range(1, npi):
                send_x_from((p + shift) % npi, ch).wait_recv()
        for source in range(npi):
            for step in range(1, fold):
                other = (y + step) % fold
                pltpu.make_async_remote_copy(
                    src_ref=all_ref.at[source, other, ch], dst_ref=all_ref.at[source, other, ch],
                    send_sem=y_send.at[source, step, ch], recv_sem=y_recv.at[source, other, ch],
                    device_id=(p, z * fold + other), device_id_type=MESH).wait_recv()
                send_y(source, ch, step).wait_send()
        for piece in range(npi):
            @pl.when((piece <= z) & (z + 1 < npi))
            def _():
                send_up(piece, ch).wait_send()

            @pl.when((piece >= z) & (z > 0))
            def _():
                send_down(piece, ch).wait_send()

            @pl.when(piece != p)
            def _():
                send_x(piece, ch).wait_send()


def contract_kernel(npi, first_i, fold, rows, nka, nj, label_ref, all_ref, ls_ref, lt_ref, out_ref,
                    as_ref, qs_ref, qt_ref, direct, crossed, left, right, cross_left, cross_right):
    p = lax.axis_index("pi")
    q = lax.axis_index("pj")
    ni = npi * rows
    nk = fold * nka
    nkp = (nk + 1) // 2
    njp = (nj + 1) // 2
    ck = all_ref.shape[3]
    nck = nka // ck
    perm = even_odd_pair()
    low = low_half((V, 2 * V))
    labels_k = [label_ref[p * nk + min(k, nk - 1)] for k in range(2 * nkp)]
    labels_i = [label_ref[first_i + i] for i in range(ni)]
    labels_j = [label_ref[q * nj + j] for j in range(nj)]

    @pl.loop(0, ni // 2)
    def _(ip):
        for kp in range(nkp):
            def block(ii, kk):
                i = 2 * ip + ii
                k = 2 * kp + kk
                if k >= nk:
                    return jnp.zeros((H, T, 2 * V), F32)
                chunk = (i % rows) * nck + (k % nka) // ck
                return split_rows(all_ref[i // rows, k // nka, chunk, (k % nka) % ck].astype(F32))

            b00, b01, b10, b11 = block(0, 0), block(0, 1), block(1, 0), block(1, 1)
            side0 = stack(b00, b10)
            side1 = stack(b01, b11)
            as_ref[ip, :, 2 * kp] = side0
            as_ref[ip, :, 2 * kp + 1] = side1
            along0 = stack(b00, b01)
            along1 = stack(b10, b11)
            for h in range(H):
                both = jnp.concatenate([side0[h], side1[h]], axis=0)
                turned = lax.dot_general(perm, both, NT, preferred_element_type=F32).astype(BF16)
                qt_ref[2 * ip, h, kp] = turned[:V]
                qt_ref[2 * ip + 1, h, kp] = turned[V:]
                both = jnp.concatenate([along0[h], along1[h]], axis=0)
                moved = lax.dot_general(both, perm, NT, preferred_element_type=F32).astype(BF16)
                qs_ref[2 * ip, h, kp] = moved[:V]
                qs_ref[2 * ip + 1, h, kp] = moved[V:]

    @pl.loop(0, H)
    def _(u):
        at = [u ^ label for label in labels_k]
        for k in range(2 * nkp):
            right[k * V:(k + 1) * V] = ls_ref[k, at[k]]
            for ip in range(ni // 2):
                cross_right[k * V:(k + 1) * V, 2 * V * ip:2 * V * (ip + 1)] = as_ref[ip, at[k], k]
        for kp in range(nkp):
            lanes = slice(2 * V * kp, 2 * V * (kp + 1))
            g0, g1 = at[2 * kp], at[2 * kp + 1]
            for i in range(ni):
                turned = jnp.where(low, qt_ref[i, g0, kp].astype(F32), qt_ref[i, g1, kp].astype(F32))
                left[i * V:(i + 1) * V, lanes] = (
                    2.0 * qs_ref[i, u ^ labels_i[i], kp].astype(F32) - turned).astype(BF16)
            for j in range(nj):
                cross_left[j * V:(j + 1) * V, lanes] = jnp.where(
                    low, lt_ref[j, g0, kp].astype(F32), lt_ref[j, g1, kp].astype(F32)).astype(BF16)
        direct[u] = jnp.dot(left[...], right[...], preferred_element_type=F32)
        crossed[u] = jnp.dot(cross_left[...], cross_right[...], preferred_element_type=F32)

    for ip in range(ni // 2):
        for jp in range(njp):
            def halves(tile):
                return pair_up(tile[:, :T], tile[:, T:])

            d = []
            for ii in range(2):
                i = 2 * ip + ii
                d.append(halves(jnp.stack(
                    [direct[h ^ labels_i[i], i * V:(i + 1) * V, 2 * V * jp:2 * V * (jp + 1)] for h in range(H)])))
            for jj in range(2):
                j = 2 * jp + jj
                if j >= nj:
                    continue
                c = halves(jnp.stack(
                    [crossed[h ^ labels_j[j], j * V:(j + 1) * V, 2 * V * ip:2 * V * (ip + 1)] for h in range(H)]))
                for ii in range(2):
                    i = 2 * ip + ii
                    out_ref[i // rows, i % rows, j] = (d[ii][jj] - c[ii]).reshape(H, V * V).astype(BF16)


def scatter_kernel(npi, part_ref, out_ref, near, sums, far, near_send, near_recv, far_send, far_recv):
    p = lax.axis_index("pi")
    q = lax.axis_index("pj")
    core = p % 2
    chip = p // 2
    chips = npi // 2
    mate = chip * 2 + 1 - core
    barrier = pltpu.get_barrier_semaphore()
    pl.semaphore_signal(barrier, inc=1, device_id=(mate, q), device_id_type=MESH)
    for step in range(1, chips):
        pl.semaphore_signal(barrier, inc=1, device_id=((chip + step) % chips * 2 + core, q), device_id_type=MESH)
    pl.semaphore_wait(barrier, chips)

    def to_mate(step):
        target = (chip + step) % chips
        return pltpu.make_async_remote_copy(
            src_ref=part_ref.at[target * 2 + 1 - core], dst_ref=near.at[step], send_sem=near_send.at[step],
            recv_sem=near_recv.at[step], device_id=(mate, q), device_id_type=MESH)

    def to_chip(step):
        return pltpu.make_async_remote_copy(
            src_ref=sums.at[step], dst_ref=far.at[step], send_sem=far_send.at[step],
            recv_sem=far_recv.at[step], device_id=((chip + step) % chips * 2 + core, q), device_id_type=MESH)

    order = [*range(1, chips), 0]
    for step in order:
        to_mate(step).start()
    for step in order:
        to_mate(step).wait_recv()
        if step:
            @pl.loop(0, out_ref.shape[0])
            def _(i):
                sums[step, i] = (part_ref[(chip + step) % chips * 2 + core, i].astype(F32)
                                 + near[step, i].astype(F32)).astype(BF16)
            to_chip(step).start()
    for step in range(1, chips):
        to_chip(step).wait_recv()

    @pl.loop(0, out_ref.shape[0])
    def _(i):
        total = part_ref[p, i].astype(F32) + near[0, i].astype(F32)
        for step in range(1, chips):
            total = total + far[step, i].astype(F32)
        out_ref[i] = total.astype(BF16)

    for step in order:
        to_mate(step).wait_send()
        if step:
            to_chip(step).wait_send()


def on_device(npi, fold, amplitudes, coulomb, exchange, occ_irrep):
    rows, nka = amplitudes.shape[:2]
    nk, nj = coulomb.shape[:2]
    nkp, njp = (nk + 1) // 2, (nj + 1) // 2
    per = 3 if nka % 3 == 0 else nka
    chunks = rows * (nka // per)
    sent = amplitudes.reshape((chunks, per) + amplitudes.shape[2:])
    vmem = pl.BlockSpec(memory_space=pltpu.VMEM)
    hbm = pl.BlockSpec(memory_space=pl.ANY)
    smem = pl.BlockSpec(memory_space=pltpu.SMEM)
    dma = pltpu.SemaphoreType.DMA
    limit = 60 * 2**20
    gathered, ls, lt = pl.pallas_call(
        functools.partial(gather_kernel, npi, fold, chunks, nk, nj),
        out_shape=(
            jax.ShapeDtypeStruct((npi, fold) + sent.shape, BF16),
            jax.ShapeDtypeStruct((2 * nkp, H, V, 2 * V * njp), BF16),
            jax.ShapeDtypeStruct((2 * njp, H, nkp, V, 2 * V), BF16),
        ),
        in_specs=[hbm, hbm, hbm],
        out_specs=(vmem, vmem, vmem),
        scratch_shapes=[
            pltpu.VMEM((npi,) + sent.shape, BF16),
            pltpu.VMEM(coulomb.shape, BF16),
            pltpu.VMEM(coulomb.shape, BF16),
            dma(()), dma(()), dma(()), dma((chunks,)),
            dma((npi, chunks)), dma((npi, chunks)), dma((npi, chunks)),
            dma((npi, chunks)), dma((npi, chunks)),
            dma((npi, fold, chunks)), dma((npi, fold, chunks)),
        ],
        compiler_params=pltpu.CompilerParams(collective_id=0, has_side_effects=True, vmem_limit_bytes=limit),
    )(sent, coulomb, exchange)
    parts = []
    span = min(npi, 8 // rows)
    ni = span * rows
    for first in range(0, npi, span):
        parts.append(pl.pallas_call(
            functools.partial(contract_kernel, span, first * rows, fold, rows, nka, nj),
            out_shape=jax.ShapeDtypeStruct((span, rows, nj) + amplitudes.shape[2:], BF16),
            in_specs=[smem, vmem, vmem, vmem],
            out_specs=vmem,
            scratch_shapes=[
                pltpu.VMEM((ni // 2, H, 2 * nkp, V, 2 * V), BF16),
                pltpu.VMEM((ni, H, nkp, V, 2 * V), BF16),
                pltpu.VMEM((ni, H, nkp, V, 2 * V), BF16),
                pltpu.VMEM((H, ni * V, 2 * V * njp), F32),
                pltpu.VMEM((H, nj * V, ni * V), F32),
                pltpu.VMEM((ni * V, 2 * nkp * V), BF16),
                pltpu.VMEM((2 * nkp * V, 2 * V * njp), BF16),
                pltpu.VMEM((nj * V, 2 * nkp * V), BF16),
                pltpu.VMEM((2 * nkp * V, ni * V), BF16),
            ],
            compiler_params=pltpu.CompilerParams(vmem_limit_bytes=limit),
        )(occ_irrep, gathered[first:first + span], ls, lt))
    parts = parts[0] if len(parts) == 1 else jnp.concatenate(parts)
    piece = (rows, nj) + amplitudes.shape[2:]
    chips = npi // 2
    return pl.pallas_call(
        functools.partial(scatter_kernel, npi),
        out_shape=jax.ShapeDtypeStruct(piece, BF16),
        in_specs=[vmem],
        out_specs=vmem,
        scratch_shapes=[
            pltpu.VMEM((chips,) + piece, BF16),
            pltpu.VMEM((chips,) + piece, BF16),
            pltpu.VMEM((chips,) + piece, BF16),
            dma((chips,)), dma((chips,)), dma((chips,)), dma((chips,)),
        ],
        compiler_params=pltpu.CompilerParams(collective_id=1, has_side_effects=True, vmem_limit_bytes=limit),
    )(parts)


def solution(mesh):
    npi, npj = mesh.shape["pi"], mesh.shape["pj"]
    placed = (P("pi", "pj", None, None), P("pi", "pj", None, None), P("pi", "pj", None, None), P())
    return jax.shard_map(
        functools.partial(on_device, npi, npj // npi), mesh=mesh, in_specs=placed,
        out_specs=P("pi", "pj", None, None), check_vma=False
    )
```

```python
import functools

import jax
import jax.numpy as jnp
from jax import lax
from jax.experimental import pallas as pl
from jax.experimental.pallas import tpu as pltpu
from jax.sharding import PartitionSpec as P

V = 64
H = 8
T = V // 2
MESH = pl.DeviceIdType.MESH
F32 = jnp.float32
BF16 = jnp.bfloat16
NT = (((1,), (1,)), ((), ()))


def even_odd_pair():
    row = lax.broadcasted_iota(jnp.int32, (2 * V, 2 * V), 0)
    col = lax.broadcasted_iota(jnp.int32, (2 * V, 2 * V), 1)
    inside = row % V
    source = (row // V) * V + 2 * (inside % T) + inside // T
    return (col == source).astype(F32).astype(BF16)


def low_half(shape):
    return lax.broadcasted_iota(jnp.int32, shape, len(shape) - 1) < V


def pair_up(first, second):
    low = low_half(first.shape)
    axis = first.ndim - 1
    return (
        jnp.where(low, first, pltpu.roll(second, V, axis)),
        jnp.where(low, pltpu.roll(first, V, axis), second),
    )


def split_rows(row):
    return row.reshape(H, T, 2 * V)


def stack(first, second):
    even, odd = pair_up(first, second)
    return jnp.concatenate([even, odd], axis=1).astype(BF16)


def ladder_part(kp, nk, nj, c_slot, x_slot, ls_ref, lt_ref):
    perm = even_odd_pair()

    def ladder(kk, j):
        return split_rows(2.0 * c_slot[kk, j].astype(F32) - x_slot[kk, j].astype(F32))

    for jp in range((nj + 1) // 2):
        tiles = []
        for kk in range(2):
            k = 2 * kp + kk
            if k >= nk:
                tile = jnp.zeros((H, V, 2 * V), BF16)
                ls_ref[k, :, :, 2 * V * jp:2 * V * (jp + 1)] = tile
                tiles.append(tile)
                continue
            first = ladder(kk, 2 * jp)
            second = ladder(kk, 2 * jp + 1) if 2 * jp + 1 < nj else jnp.zeros_like(first)
            tile = stack(first, second)
            ls_ref[k, :, :, 2 * V * jp:2 * V * (jp + 1)] = tile
            tiles.append(tile)
        for h in range(H):
            both = jnp.concatenate([tiles[0][h], tiles[1][h]], axis=0)
            turned = lax.dot_general(perm, both, NT, preferred_element_type=F32).astype(BF16)
            lt_ref[2 * jp, h, kp] = turned[:V]
            lt_ref[2 * jp + 1, h, kp] = turned[V:]


def gather(npi, fold, chunks, nk, nj, use, amp_ref, c_hbm, x_hbm, all_ref, ls_ref, lt_ref,
                  col, c_ref, x_ref, c_sem, x_sem, own_sem, local_sem, col_recv, up_send, down_send,
                  x_recv, x_send, y_recv, y_send):
    p = lax.axis_index("pi")
    q = lax.axis_index("pj")
    z = q // fold
    y = q % fold
    barrier = pltpu.get_barrier_semaphore()
    up = (p, q + fold)
    down = (p, q - fold)

    @pl.when(z + 1 < npi)
    def _():
        pl.semaphore_signal(barrier, inc=1, device_id=up, device_id_type=MESH)

    @pl.when(z > 0)
    def _():
        pl.semaphore_signal(barrier, inc=1, device_id=down, device_id_type=MESH)

    for step in range(1, npi):
        pl.semaphore_signal(barrier, inc=1, device_id=((p + step) % npi, q), device_id_type=MESH)
    for step in range(1, fold):
        pl.semaphore_signal(barrier, inc=1, device_id=(p, z * fold + (y + step) % fold), device_id_type=MESH)

    nkp = (nk + 1) // 2

    def loads(kp):
        slot, count = kp % 2, min(2, nk - 2 * kp)
        return (
            pltpu.make_async_copy(c_hbm.at[pl.ds(2 * kp, count)], c_ref.at[slot, pl.ds(0, count)], c_sem.at[slot]),
            pltpu.make_async_copy(x_hbm.at[pl.ds(2 * kp, count)], x_ref.at[slot, pl.ds(0, count)], x_sem.at[slot]),
        )

    own = pltpu.make_async_copy(amp_ref, col.at[z], own_sem)
    own.start()
    for kp in range(min(2, nkp)):
        for load in loads(kp):
            load.start()

    at_end = (z == 0) | (z == npi - 1)

    @pl.when(at_end)
    def _():
        pl.semaphore_wait(barrier, npi + fold - 1)

    @pl.when(jnp.logical_not(at_end))
    def _():
        pl.semaphore_wait(barrier, npi + fold)

    own.wait()

    def send_up(piece, ch):
        return pltpu.make_async_remote_copy(
            src_ref=col.at[piece, ch], dst_ref=col.at[piece, ch], send_sem=up_send.at[piece, ch],
            recv_sem=col_recv.at[piece, ch], device_id=up, device_id_type=MESH)

    def send_down(piece, ch):
        return pltpu.make_async_remote_copy(
            src_ref=col.at[piece, ch], dst_ref=col.at[piece, ch], send_sem=down_send.at[piece, ch],
            recv_sem=col_recv.at[piece, ch], device_id=down, device_id_type=MESH)

    def send_x(piece, ch):
        return pltpu.make_async_remote_copy(
            src_ref=col.at[piece, ch], dst_ref=all_ref.at[p, y, ch], send_sem=x_send.at[piece, ch],
            recv_sem=x_recv.at[p, ch], device_id=(piece, q), device_id_type=MESH)

    def keep(ch):
        return pltpu.make_async_copy(col.at[p, ch], all_ref.at[p, y, ch], local_sem.at[ch])

    def send_y(source, ch, step):
        return pltpu.make_async_remote_copy(
            src_ref=all_ref.at[source, y, ch], dst_ref=all_ref.at[source, y, ch],
            send_sem=y_send.at[source, step, ch], recv_sem=y_recv.at[source, y, ch],
            device_id=(p, z * fold + (y + step) % fold), device_id_type=MESH)

    def send_own_y(ch, step):
        return pltpu.make_async_remote_copy(
            src_ref=col.at[p, ch], dst_ref=all_ref.at[p, y, ch],
            send_sem=y_send.at[p, step, ch], recv_sem=y_recv.at[p, y, ch],
            device_id=(p, z * fold + (y + step) % fold), device_id_type=MESH)

    def place(piece, ch):
        @pl.when(piece != p)
        def _():
            send_x(piece, ch).start()

        @pl.when(piece == p)
        def _():
            keep(ch).start()
            for step in range(1, fold):
                send_own_y(ch, step).start()

    away = jnp.where(z > p, z - p, p - z)
    lag = 2

    def forward_y(event):
        if fold > 1 and 0 <= event < npi * chunks:
            ch = event % chunks

            @pl.when(away == event // chunks)
            def _():
                for shift in range(1, npi):
                    source = (p + shift) % npi
                    send_x_from(source, ch).wait_recv()
                    for step in range(1, fold):
                        send_y(source, ch, step).start()

    def send_x_from(source, ch):
        return pltpu.make_async_remote_copy(
            src_ref=col.at[0, ch], dst_ref=all_ref.at[source, y, ch], send_sem=x_send.at[0, ch],
            recv_sem=x_recv.at[source, ch], device_id=(source, q), device_id_type=MESH)

    for ch in range(chunks):
        @pl.when(z + 1 < npi)
        def _():
            send_up(z, ch).start()

        @pl.when(z > 0)
        def _():
            send_down(z, ch).start()

        place(z, ch)

    parts = list(range(nkp))

    def some_ladder():
        if parts:
            kp = parts.pop(0)
            for load in loads(kp):
                load.wait()
            ladder_part(kp, nk, nj, c_ref.at[kp % 2], x_ref.at[kp % 2], ls_ref, lt_ref)
            if kp + 2 < nkp:
                for load in loads(kp + 2):
                    load.start()

    some_ladder()
    for event in range(chunks, npi * chunks):
        far, ch = event // chunks, event % chunks
        below = z - far
        above = z + far

        @pl.when(below >= 0)
        def _():
            send_up(below, ch).wait_recv()

            @pl.when(z + 1 < npi)
            def _():
                send_up(below, ch).start()

            place(below, ch)

        @pl.when(above < npi)
        def _():
            send_down(above, ch).wait_recv()

            @pl.when(z > 0)
            def _():
                send_down(above, ch).start()

            place(above, ch)

        if event == chunks:
            for early in range(chunks - lag):
                forward_y(early)
        forward_y(event - lag)
        some_ladder()
    while parts:
        some_ladder()
    for late in range(npi * chunks - lag, npi * chunks):
        forward_y(late)

    for ch in range(chunks):
        keep(ch).wait()
        if fold == 1:
            for shift in range(1, npi):
                send_x_from((p + shift) % npi, ch).wait_recv()
    use(0)
    for half in range(1, fold):
        other = (y + half) % fold
        for ch in range(chunks):
            for source in range(npi):
                pltpu.make_async_remote_copy(
                    src_ref=all_ref.at[source, other, ch], dst_ref=all_ref.at[source, other, ch],
                    send_sem=y_send.at[source, half, ch], recv_sem=y_recv.at[source, other, ch],
                    device_id=(p, z * fold + other), device_id_type=MESH).wait_recv()
        use(half)

    for ch in range(chunks):
        for source in range(npi):
            for step in range(1, fold):
                send_y(source, ch, step).wait_send()
        for piece in range(npi):
            @pl.when((piece <= z) & (z + 1 < npi))
            def _():
                send_up(piece, ch).wait_send()

            @pl.when((piece >= z) & (z > 0))
            def _():
                send_down(piece, ch).wait_send()

            @pl.when(piece != p)
            def _():
                send_x(piece, ch).wait_send()


def gather_kernel(npi, fold, chunks, nk, nj, *refs):
    gather(npi, fold, chunks, nk, nj, lambda half: None, *refs)


def fused_kernel(npi, fold, chunks, nk, nj, rows, nka, label_ref, amp_ref, c_hbm, x_hbm, out_ref,
                 all_ref, ls_ref, lt_ref, *scratch):
    held = len(scratch) - 9
    steps = contraction(npi, 0, fold, rows, nka, nj, label_ref, all_ref, ls_ref, lt_ref, out_ref, *scratch[held:])

    def use(half):
        steps[0](half)
        if half == fold - 1:
            steps[1]()

    gather(npi, fold, chunks, nk, nj, use, amp_ref, c_hbm, x_hbm, all_ref, ls_ref, lt_ref, *scratch[:held])


def contract_kernel(npi, first_i, fold, *rest):
    steps = contraction(npi, first_i, fold, *rest)
    for half in range(fold):
        steps[0](half)
    steps[1]()


def contraction(npi, first_i, fold, rows, nka, nj, label_ref, all_ref, ls_ref, lt_ref, out_ref,
                as_ref, qs_ref, qt_ref, direct, crossed, left, right, cross_left, cross_right):
    p = lax.axis_index("pi")
    q = lax.axis_index("pj")
    y = q % fold
    ni = npi * rows
    nkp = (nka + 1) // 2
    njp = (nj + 1) // 2
    ck = all_ref.shape[3]
    nck = nka // ck
    labels_i = [label_ref[first_i + i] for i in range(ni)]
    labels_j = [label_ref[q * nj + j] for j in range(nj)]

    def add(half):
        part = (y + half) % fold
        perm = even_odd_pair()
        low = low_half((V, 2 * V))
        labels_k = [label_ref[(p * fold + part) * nka + min(k, nka - 1)] for k in range(2 * nkp)]

        @pl.loop(0, ni // 2)
        def _(ip):
            for kp in range(nkp):
                def block(ii, kk):
                    i = 2 * ip + ii
                    k = 2 * kp + kk
                    if k >= nka:
                        return jnp.zeros((H, T, 2 * V), F32)
                    chunk = (i % rows) * nck + k // ck
                    return split_rows(all_ref[i // rows, part, chunk, k % ck].astype(F32))

                b00, b01, b10, b11 = block(0, 0), block(0, 1), block(1, 0), block(1, 1)
                side0 = stack(b00, b10)
                side1 = stack(b01, b11)
                as_ref[ip, :, 2 * kp] = side0
                as_ref[ip, :, 2 * kp + 1] = side1
                along0 = stack(b00, b01)
                along1 = stack(b10, b11)
                for h in range(H):
                    both = jnp.concatenate([side0[h], side1[h]], axis=0)
                    turned = lax.dot_general(perm, both, NT, preferred_element_type=F32).astype(BF16)
                    qt_ref[2 * ip, h, kp] = turned[:V]
                    qt_ref[2 * ip + 1, h, kp] = turned[V:]
                    both = jnp.concatenate([along0[h], along1[h]], axis=0)
                    moved = lax.dot_general(both, perm, NT, preferred_element_type=F32).astype(BF16)
                    qs_ref[2 * ip, h, kp] = moved[:V]
                    qs_ref[2 * ip + 1, h, kp] = moved[V:]

        @pl.loop(0, H)
        def _(u):
            at = [u ^ label for label in labels_k]
            for k in range(2 * nkp):
                right[k * V:(k + 1) * V] = ls_ref[part * 2 * nkp + k, at[k]]
                for ip in range(ni // 2):
                    cross_right[k * V:(k + 1) * V, 2 * V * ip:2 * V * (ip + 1)] = as_ref[ip, at[k], k]
            for kp in range(nkp):
                lanes = slice(2 * V * kp, 2 * V * (kp + 1))
                g0, g1 = at[2 * kp], at[2 * kp + 1]
                for i in range(ni):
                    turned = jnp.where(low, qt_ref[i, g0, kp].astype(F32), qt_ref[i, g1, kp].astype(F32))
                    left[i * V:(i + 1) * V, lanes] = (
                        2.0 * qs_ref[i, u ^ labels_i[i], kp].astype(F32) - turned).astype(BF16)
                for j in range(nj):
                    from_k = part * nkp + kp
                    cross_left[j * V:(j + 1) * V, lanes] = jnp.where(
                        low, lt_ref[j, g0, from_k].astype(F32), lt_ref[j, g1, from_k].astype(F32)).astype(BF16)
            added = jnp.dot(left[...], right[...], preferred_element_type=F32)
            direct[u] = direct[u] + added if half else added
            added = jnp.dot(cross_left[...], cross_right[...], preferred_element_type=F32)
            crossed[u] = crossed[u] + added if half else added

    def finish():
        for ip in range(ni // 2):
            for jp in range(njp):
                def halves(tile):
                    return pair_up(tile[:, :T], tile[:, T:])

                d = []
                for ii in range(2):
                    i = 2 * ip + ii
                    d.append(halves(jnp.stack(
                        [direct[h ^ labels_i[i], i * V:(i + 1) * V, 2 * V * jp:2 * V * (jp + 1)] for h in range(H)])))
                for jj in range(2):
                    j = 2 * jp + jj
                    if j >= nj:
                        continue
                    c = halves(jnp.stack(
                        [crossed[h ^ labels_j[j], j * V:(j + 1) * V, 2 * V * ip:2 * V * (ip + 1)] for h in range(H)]))
                    for ii in range(2):
                        i = 2 * ip + ii
                        out_ref[i // rows, i % rows, j] = (d[ii][jj] - c[ii]).reshape(H, V * V).astype(BF16)

    return add, finish


def scatter_kernel(npi, part_ref, out_ref, near, sums, far, near_send, near_recv, far_send, far_recv):
    p = lax.axis_index("pi")
    q = lax.axis_index("pj")
    core = p % 2
    chip = p // 2
    chips = npi // 2
    mate = chip * 2 + 1 - core
    barrier = pltpu.get_barrier_semaphore()
    pl.semaphore_signal(barrier, inc=1, device_id=(mate, q), device_id_type=MESH)
    for step in range(1, chips):
        pl.semaphore_signal(barrier, inc=1, device_id=((chip + step) % chips * 2 + core, q), device_id_type=MESH)
    pl.semaphore_wait(barrier, chips)

    def to_mate(step):
        target = (chip + step) % chips
        return pltpu.make_async_remote_copy(
            src_ref=part_ref.at[target * 2 + 1 - core], dst_ref=near.at[step], send_sem=near_send.at[step],
            recv_sem=near_recv.at[step], device_id=(mate, q), device_id_type=MESH)

    def to_chip(step):
        return pltpu.make_async_remote_copy(
            src_ref=sums.at[step], dst_ref=far.at[step], send_sem=far_send.at[step],
            recv_sem=far_recv.at[step], device_id=((chip + step) % chips * 2 + core, q), device_id_type=MESH)

    order = [*range(1, chips), 0]
    for step in order:
        to_mate(step).start()
    for step in order:
        to_mate(step).wait_recv()
        if step:
            @pl.loop(0, out_ref.shape[0])
            def _(i):
                sums[step, i] = (part_ref[(chip + step) % chips * 2 + core, i].astype(F32)
                                 + near[step, i].astype(F32)).astype(BF16)
            to_chip(step).start()
    for step in range(1, chips):
        to_chip(step).wait_recv()

    @pl.loop(0, out_ref.shape[0])
    def _(i):
        total = part_ref[p, i].astype(F32) + near[0, i].astype(F32)
        for step in range(1, chips):
            total = total + far[step, i].astype(F32)
        out_ref[i] = total.astype(BF16)

    for step in order:
        to_mate(step).wait_send()
        if step:
            to_chip(step).wait_send()


def on_device(npi, fold, amplitudes, coulomb, exchange, occ_irrep):
    rows, nka = amplitudes.shape[:2]
    nk, nj = coulomb.shape[:2]
    nkp, njp = (nk + 1) // 2, (nj + 1) // 2
    per = 3 if nka % 3 == 0 else nka
    chunks = rows * (nka // per)
    sent = amplitudes.reshape((chunks, per) + amplitudes.shape[2:])
    vmem = pl.BlockSpec(memory_space=pltpu.VMEM)
    hbm = pl.BlockSpec(memory_space=pl.ANY)
    smem = pl.BlockSpec(memory_space=pltpu.SMEM)
    dma = pltpu.SemaphoreType.DMA
    limit = 60 * 2**20
    assert fold == 1 or nka % 2 == 0
    held = [
        pltpu.VMEM((npi,) + sent.shape, BF16),
        pltpu.VMEM((2, 2) + coulomb.shape[1:], BF16),
        pltpu.VMEM((2, 2) + coulomb.shape[1:], BF16),
        dma((2,)), dma((2,)), dma(()), dma((chunks,)),
        dma((npi, chunks)), dma((npi, chunks)), dma((npi, chunks)),
        dma((npi, chunks)), dma((npi, chunks)),
        dma((npi, fold, chunks)), dma((npi, fold, chunks)),
    ]
    shared = [
        ((npi, fold) + sent.shape, BF16),
        ((2 * nkp, H, V, 2 * V * njp), BF16),
        ((2 * njp, H, nkp, V, 2 * V), BF16),
    ]
    span = min(npi, 8 // rows)
    ni = span * rows
    half = (nka + 1) // 2
    worked = [
        pltpu.VMEM((ni // 2, H, 2 * half, V, 2 * V), BF16),
        pltpu.VMEM((ni, H, half, V, 2 * V), BF16),
        pltpu.VMEM((ni, H, half, V, 2 * V), BF16),
        pltpu.VMEM((H, ni * V, 2 * V * njp), F32),
        pltpu.VMEM((H, nj * V, ni * V), F32),
        pltpu.VMEM((ni * V, 2 * half * V), BF16),
        pltpu.VMEM((2 * half * V, 2 * V * njp), BF16),
        pltpu.VMEM((nj * V, 2 * half * V), BF16),
        pltpu.VMEM((2 * half * V, ni * V), BF16),
    ]
    reach = pltpu.CompilerParams(collective_id=0, has_side_effects=True, vmem_limit_bytes=limit)
    if span == npi:
        parts = pl.pallas_call(
            functools.partial(fused_kernel, npi, fold, chunks, nk, nj, rows, nka),
            out_shape=jax.ShapeDtypeStruct((npi, rows, nj) + amplitudes.shape[2:], BF16),
            in_specs=[smem, hbm, hbm, hbm],
            out_specs=vmem,
            scratch_shapes=[pltpu.VMEM(*one) for one in shared] + held + worked,
            compiler_params=reach,
        )(occ_irrep, sent, coulomb, exchange)
    else:
        gathered, ls, lt = pl.pallas_call(
            functools.partial(gather_kernel, npi, fold, chunks, nk, nj),
            out_shape=[jax.ShapeDtypeStruct(*one) for one in shared],
            in_specs=[hbm, hbm, hbm],
            out_specs=[vmem, vmem, vmem],
            scratch_shapes=held,
            compiler_params=reach,
        )(sent, coulomb, exchange)
        parts = jnp.concatenate([
            pl.pallas_call(
                functools.partial(contract_kernel, span, first * rows, fold, rows, nka, nj),
                out_shape=jax.ShapeDtypeStruct((span, rows, nj) + amplitudes.shape[2:], BF16),
                in_specs=[smem, vmem, vmem, vmem],
                out_specs=vmem,
                scratch_shapes=worked,
                compiler_params=pltpu.CompilerParams(vmem_limit_bytes=limit),
            )(occ_irrep, gathered[first:first + span], ls, lt)
            for first in range(0, npi, span)
        ])
    piece = (rows, nj) + amplitudes.shape[2:]
    chips = npi // 2
    return pl.pallas_call(
        functools.partial(scatter_kernel, npi),
        out_shape=jax.ShapeDtypeStruct(piece, BF16),
        in_specs=[vmem],
        out_specs=vmem,
        scratch_shapes=[
            pltpu.VMEM((chips,) + piece, BF16),
            pltpu.VMEM((chips,) + piece, BF16),
            pltpu.VMEM((chips,) + piece, BF16),
            dma((chips,)), dma((chips,)), dma((chips,)), dma((chips,)),
        ],
        compiler_params=pltpu.CompilerParams(collective_id=1, has_side_effects=True, vmem_limit_bytes=limit),
    )(parts)


def solution(mesh):
    npi, npj = mesh.shape["pi"], mesh.shape["pj"]
    placed = (P("pi", "pj", None, None), P("pi", "pj", None, None), P("pi", "pj", None, None), P())
    return jax.shard_map(
        functools.partial(on_device, npi, npj // npi), mesh=mesh, in_specs=placed,
        out_specs=P("pi", "pj", None, None), check_vma=False
    )
```

```python
import functools

import jax
import jax.numpy as jnp
from jax import lax
from jax.experimental import pallas as pl
from jax.experimental.pallas import tpu as pltpu
from jax.sharding import PartitionSpec as P

V = 64
H = 8
T = V // 2
MESH = pl.DeviceIdType.MESH
F32 = jnp.float32
BF16 = jnp.bfloat16
NT = (((1,), (1,)), ((), ()))


def even_odd_pair():
    row = lax.broadcasted_iota(jnp.int32, (2 * V, 2 * V), 0)
    col = lax.broadcasted_iota(jnp.int32, (2 * V, 2 * V), 1)
    inside = row % V
    source = (row // V) * V + 2 * (inside % T) + inside // T
    return (col == source).astype(F32).astype(BF16)


def low_half(shape):
    return lax.broadcasted_iota(jnp.int32, shape, len(shape) - 1) < V


def pair_up(first, second):
    low = low_half(first.shape)
    axis = first.ndim - 1
    return (
        jnp.where(low, first, pltpu.roll(second, V, axis)),
        jnp.where(low, pltpu.roll(first, V, axis), second),
    )


def split_rows(row):
    return row.reshape(H, T, 2 * V)


def stack(first, second):
    even, odd = pair_up(first, second)
    return jnp.concatenate([even, odd], axis=1).astype(BF16)


def ladder_part(kp, nk, nj, c_slot, x_slot, ls_ref, lt_ref):
    perm = even_odd_pair()

    def ladder(kk, j):
        return split_rows(2.0 * c_slot[kk, j].astype(F32) - x_slot[kk, j].astype(F32))

    for jp in range((nj + 1) // 2):
        tiles = []
        for kk in range(2):
            k = 2 * kp + kk
            if k >= nk:
                tile = jnp.zeros((H, V, 2 * V), BF16)
                ls_ref[k, :, :, 2 * V * jp:2 * V * (jp + 1)] = tile
                tiles.append(tile)
                continue
            first = ladder(kk, 2 * jp)
            second = ladder(kk, 2 * jp + 1) if 2 * jp + 1 < nj else jnp.zeros_like(first)
            tile = stack(first, second)
            ls_ref[k, :, :, 2 * V * jp:2 * V * (jp + 1)] = tile
            tiles.append(tile)
        for h in range(H):
            both = jnp.concatenate([tiles[0][h], tiles[1][h]], axis=0)
            turned = lax.dot_general(perm, both, NT, preferred_element_type=F32).astype(BF16)
            lt_ref[2 * jp, h, kp] = turned[:V]
            lt_ref[2 * jp + 1, h, kp] = turned[V:]


def gather(npi, fold, chunks, nk, nj, use, amp_ref, c_hbm, x_hbm, all_ref, ls_ref, lt_ref,
                  col, c_ref, x_ref, c_sem, x_sem, own_sem, local_sem, col_recv, up_send, down_send,
                  x_recv, x_send, y_recv, y_send,
           swapped, swap_send, swap_recv, pass_send, side_recv, side_send, side_keep):
    p = lax.axis_index("pi")
    q = lax.axis_index("pj")
    z = q // fold
    y = q % fold
    barrier = pltpu.get_barrier_semaphore()
    up = (p, q + fold)
    down = (p, q - fold)

    @pl.when(z + 1 < npi)
    def _():
        pl.semaphore_signal(barrier, inc=1, device_id=up, device_id_type=MESH)

    @pl.when(z > 0)
    def _():
        pl.semaphore_signal(barrier, inc=1, device_id=down, device_id_type=MESH)

    for step in range(1, npi):
        pl.semaphore_signal(barrier, inc=1, device_id=((p + step) % npi, q), device_id_type=MESH)
    for step in range(1, fold):
        pl.semaphore_signal(barrier, inc=1, device_id=(p, z * fold + (y + step) % fold), device_id_type=MESH)

    nkp = (nk + 1) // 2

    def loads(kp):
        slot, count = kp % 2, min(2, nk - 2 * kp)
        return (
            pltpu.make_async_copy(c_hbm.at[pl.ds(2 * kp, count)], c_ref.at[slot, pl.ds(0, count)], c_sem.at[slot]),
            pltpu.make_async_copy(x_hbm.at[pl.ds(2 * kp, count)], x_ref.at[slot, pl.ds(0, count)], x_sem.at[slot]),
        )

    own = pltpu.make_async_copy(amp_ref, col.at[z], own_sem)
    own.start()
    for kp in range(min(2, nkp)):
        for load in loads(kp):
            load.start()

    at_end = (z == 0) | (z == npi - 1)

    @pl.when(at_end)
    def _():
        pl.semaphore_wait(barrier, npi + fold - 1)

    @pl.when(jnp.logical_not(at_end))
    def _():
        pl.semaphore_wait(barrier, npi + fold)

    own.wait()

    def send_up(piece, ch):
        return pltpu.make_async_remote_copy(
            src_ref=col.at[piece, ch], dst_ref=col.at[piece, ch], send_sem=up_send.at[piece, ch],
            recv_sem=col_recv.at[piece, ch], device_id=up, device_id_type=MESH)

    def send_down(piece, ch):
        return pltpu.make_async_remote_copy(
            src_ref=col.at[piece, ch], dst_ref=col.at[piece, ch], send_sem=down_send.at[piece, ch],
            recv_sem=col_recv.at[piece, ch], device_id=down, device_id_type=MESH)

    def send_x(piece, ch):
        return pltpu.make_async_remote_copy(
            src_ref=col.at[piece, ch], dst_ref=all_ref.at[p, y, ch], send_sem=x_send.at[piece, ch],
            recv_sem=x_recv.at[p, ch], device_id=(piece, q), device_id_type=MESH)

    def keep(ch):
        return pltpu.make_async_copy(col.at[p, ch], all_ref.at[p, y, ch], local_sem.at[ch])

    def send_y(source, ch, step):
        return pltpu.make_async_remote_copy(
            src_ref=all_ref.at[source, y, ch], dst_ref=all_ref.at[source, y, ch],
            send_sem=y_send.at[source, step, ch], recv_sem=y_recv.at[source, y, ch],
            device_id=(p, z * fold + (y + step) % fold), device_id_type=MESH)

    early = list(range(chunks // 2, chunks)) if fold == 2 else []
    ends = (0, npi - 1)
    inner = (p > 0) & (p < npi - 1)
    across = (p, z * fold + (y + 1) % fold)

    def swap(end, ch):
        return pltpu.make_async_remote_copy(
            src_ref=col.at[ends[end], ch], dst_ref=swapped.at[end, early.index(ch)],
            send_sem=swap_send.at[end, early.index(ch)], recv_sem=swap_recv.at[end, early.index(ch)],
            device_id=across, device_id_type=MESH)

    def pass_on(end, ch):
        at = early.index(ch)
        return pltpu.make_async_remote_copy(
            src_ref=swapped.at[end, at], dst_ref=swapped.at[end, at], send_sem=pass_send.at[end, at],
            recv_sem=swap_recv.at[end, at], device_id=down if end else up, device_id_type=MESH)

    def send_side(end, ch):
        at = early.index(ch)
        return pltpu.make_async_remote_copy(
            src_ref=swapped.at[end, at], dst_ref=all_ref.at[p, (y + 1) % fold, ch], send_sem=side_send.at[end, at],
            recv_sem=side_recv.at[p, at], device_id=(ends[end], q), device_id_type=MESH)

    def side_from(source, ch):
        at = early.index(ch)
        return pltpu.make_async_remote_copy(
            src_ref=swapped.at[0, at], dst_ref=all_ref.at[source, (y + 1) % fold, ch], send_sem=side_send.at[0, at],
            recv_sem=side_recv.at[source, at], device_id=(source, q), device_id_type=MESH)

    def keep_side(end, ch):
        at = early.index(ch)
        return pltpu.make_async_copy(swapped.at[end, at], all_ref.at[p, (y + 1) % fold, ch], side_keep.at[at])

    def passes(end):
        return z > 0 if end else z + 1 < npi

    def place_side(end, ch):
        swap(end, ch).wait_recv()

        @pl.when(passes(end))
        def _():
            pass_on(end, ch).start()

        @pl.when(p != ends[end])
        def _():
            send_side(end, ch).start()

        @pl.when(p == ends[end])
        def _():
            keep_side(end, ch).start()

    def send_own_y(ch, step):
        return pltpu.make_async_remote_copy(
            src_ref=col.at[p, ch], dst_ref=all_ref.at[p, y, ch],
            send_sem=y_send.at[p, step, ch], recv_sem=y_recv.at[p, y, ch],
            device_id=(p, z * fold + (y + step) % fold), device_id_type=MESH)

    def place(piece, ch):
        @pl.when(piece != p)
        def _():
            send_x(piece, ch).start()

        @pl.when(piece == p)
        def _():
            keep(ch).start()

        @pl.when((piece == p) & (inner | (ch not in early)))
        def _():
            for step in range(1, fold):
                send_own_y(ch, step).start()

    away = jnp.where(z > p, z - p, p - z)
    lag = 2

    def forward_y(event):
        if fold > 1 and 0 <= event < npi * chunks:
            ch = event % chunks

            @pl.when(away == event // chunks)
            def _():
                for shift in range(1, npi):
                    source = (p + shift) % npi
                    send_x_from(source, ch).wait_recv()

                    @pl.when(inner | (ch not in early))
                    def _():
                        for step in range(1, fold):
                            send_y(source, ch, step).start()

    def send_x_from(source, ch):
        return pltpu.make_async_remote_copy(
            src_ref=col.at[0, ch], dst_ref=all_ref.at[source, y, ch], send_sem=x_send.at[0, ch],
            recv_sem=x_recv.at[source, ch], device_id=(source, q), device_id_type=MESH)

    for ch in range(chunks):
        @pl.when(z + 1 < npi)
        def _():
            send_up(z, ch).start()

        @pl.when(z > 0)
        def _():
            send_down(z, ch).start()

        if ch in early:
            for end in range(2):
                @pl.when(z == ends[end])
                def _():
                    swap(end, ch).start()

        place(z, ch)

    parts = list(range(nkp))

    def some_ladder():
        if parts:
            kp = parts.pop(0)
            for load in loads(kp):
                load.wait()
            ladder_part(kp, nk, nj, c_ref.at[kp % 2], x_ref.at[kp % 2], ls_ref, lt_ref)
            if kp + 2 < nkp:
                for load in loads(kp + 2):
                    load.start()

    some_ladder()
    for event in range(chunks, npi * chunks):
        far, ch = event // chunks, event % chunks
        below = z - far
        above = z + far

        @pl.when(below >= 0)
        def _():
            send_up(below, ch).wait_recv()

            @pl.when(z + 1 < npi)
            def _():
                send_up(below, ch).start()

            place(below, ch)

        @pl.when(above < npi)
        def _():
            send_down(above, ch).wait_recv()

            @pl.when(z > 0)
            def _():
                send_down(above, ch).start()

            place(above, ch)

        if ch in early:
            @pl.when(below == 0)
            def _():
                place_side(0, ch)

            @pl.when(above == npi - 1)
            def _():
                place_side(1, ch)

        if far == 1 and chunks - 1 - ch in early:
            for end in range(2):
                @pl.when(z == ends[end])
                def _():
                    place_side(end, early[ch])

        if event == chunks:
            for first in range(chunks - lag):
                forward_y(first)
        forward_y(event - lag)
        some_ladder()
    while parts:
        some_ladder()
    for late in range(npi * chunks - lag, npi * chunks):
        forward_y(late)

    for ch in range(chunks):
        keep(ch).wait()
        if fold == 1:
            for shift in range(1, npi):
                send_x_from((p + shift) % npi, ch).wait_recv()
    use(0)
    for half in range(1, fold):
        other = (y + half) % fold
        for ch in range(chunks):
            @pl.when(inner | (ch not in early))
            def _():
                for source in range(npi):
                    pltpu.make_async_remote_copy(
                        src_ref=all_ref.at[source, other, ch], dst_ref=all_ref.at[source, other, ch],
                        send_sem=y_send.at[source, half, ch], recv_sem=y_recv.at[source, other, ch],
                        device_id=(p, z * fold + other), device_id_type=MESH).wait_recv()

            if ch in early:
                @pl.when(jnp.logical_not(inner))
                def _():
                    for shift in range(1, npi):
                        side_from((p + shift) % npi, ch).wait_recv()
                    keep_side(0, ch).wait()

        use(half)

    for ch in range(chunks):
        @pl.when(inner | (ch not in early))
        def _():
            for source in range(npi):
                for step in range(1, fold):
                    send_y(source, ch, step).wait_send()

        if ch in early:
            for end in range(2):
                @pl.when(z == ends[end])
                def _():
                    swap(end, ch).wait_send()

                @pl.when(passes(end))
                def _():
                    pass_on(end, ch).wait_send()

                @pl.when(p != ends[end])
                def _():
                    send_side(end, ch).wait_send()

        for piece in range(npi):
            @pl.when((piece <= z) & (z + 1 < npi))
            def _():
                send_up(piece, ch).wait_send()

            @pl.when((piece >= z) & (z > 0))
            def _():
                send_down(piece, ch).wait_send()

            @pl.when(piece != p)
            def _():
                send_x(piece, ch).wait_send()


def gather_kernel(npi, fold, chunks, nk, nj, *refs):
    gather(npi, fold, chunks, nk, nj, lambda half: None, *refs)


def fused_kernel(npi, fold, chunks, nk, nj, rows, nka, label_ref, amp_ref, c_hbm, x_hbm, out_ref,
                 all_ref, ls_ref, lt_ref, *scratch):
    held = len(scratch) - 9
    steps = contraction(npi, 0, fold, rows, nka, nj, label_ref, all_ref, ls_ref, lt_ref, out_ref, *scratch[held:])

    def use(half):
        steps[0](half)
        if half == fold - 1:
            steps[1]()

    gather(npi, fold, chunks, nk, nj, use, amp_ref, c_hbm, x_hbm, all_ref, ls_ref, lt_ref, *scratch[:held])


def contract_kernel(npi, first_i, fold, *rest):
    steps = contraction(npi, first_i, fold, *rest)
    for half in range(fold):
        steps[0](half)
    steps[1]()


def contraction(npi, first_i, fold, rows, nka, nj, label_ref, all_ref, ls_ref, lt_ref, out_ref,
                as_ref, qs_ref, qt_ref, direct, crossed, left, right, cross_left, cross_right):
    p = lax.axis_index("pi")
    q = lax.axis_index("pj")
    y = q % fold
    ni = npi * rows
    nkp = (nka + 1) // 2
    njp = (nj + 1) // 2
    ck = all_ref.shape[3]
    nck = nka // ck
    labels_i = [label_ref[first_i + i] for i in range(ni)]
    labels_j = [label_ref[q * nj + j] for j in range(nj)]

    def add(half):
        part = (y + half) % fold
        perm = even_odd_pair()
        low = low_half((V, 2 * V))
        labels_k = [label_ref[(p * fold + part) * nka + min(k, nka - 1)] for k in range(2 * nkp)]

        @pl.loop(0, ni // 2)
        def _(ip):
            for kp in range(nkp):
                def block(ii, kk):
                    i = 2 * ip + ii
                    k = 2 * kp + kk
                    if k >= nka:
                        return jnp.zeros((H, T, 2 * V), F32)
                    chunk = (i % rows) * nck + k // ck
                    return split_rows(all_ref[i // rows, part, chunk, k % ck].astype(F32))

                b00, b01, b10, b11 = block(0, 0), block(0, 1), block(1, 0), block(1, 1)
                side0 = stack(b00, b10)
                side1 = stack(b01, b11)
                as_ref[ip, :, 2 * kp] = side0
                as_ref[ip, :, 2 * kp + 1] = side1
                along0 = stack(b00, b01)
                along1 = stack(b10, b11)
                for h in range(H):
                    both = jnp.concatenate([side0[h], side1[h]], axis=0)
                    turned = lax.dot_general(perm, both, NT, preferred_element_type=F32).astype(BF16)
                    qt_ref[2 * ip, h, kp] = turned[:V]
                    qt_ref[2 * ip + 1, h, kp] = turned[V:]
                    both = jnp.concatenate([along0[h], along1[h]], axis=0)
                    moved = lax.dot_general(both, perm, NT, preferred_element_type=F32).astype(BF16)
                    qs_ref[2 * ip, h, kp] = moved[:V]
                    qs_ref[2 * ip + 1, h, kp] = moved[V:]

        @pl.loop(0, H)
        def _(u):
            at = [u ^ label for label in labels_k]
            for k in range(2 * nkp):
                right[k * V:(k + 1) * V] = ls_ref[part * 2 * nkp + k, at[k]]
                for ip in range(ni // 2):
                    cross_right[k * V:(k + 1) * V, 2 * V * ip:2 * V * (ip + 1)] = as_ref[ip, at[k], k]
            for kp in range(nkp):
                lanes = slice(2 * V * kp, 2 * V * (kp + 1))
                g0, g1 = at[2 * kp], at[2 * kp + 1]
                for i in range(ni):
                    turned = jnp.where(low, qt_ref[i, g0, kp].astype(F32), qt_ref[i, g1, kp].astype(F32))
                    left[i * V:(i + 1) * V, lanes] = (
                        2.0 * qs_ref[i, u ^ labels_i[i], kp].astype(F32) - turned).astype(BF16)
                for j in range(nj):
                    from_k = part * nkp + kp
                    cross_left[j * V:(j + 1) * V, lanes] = jnp.where(
                        low, lt_ref[j, g0, from_k].astype(F32), lt_ref[j, g1, from_k].astype(F32)).astype(BF16)
            added = jnp.dot(left[...], right[...], preferred_element_type=F32)
            direct[u] = direct[u] + added if half else added
            added = jnp.dot(cross_left[...], cross_right[...], preferred_element_type=F32)
            crossed[u] = crossed[u] + added if half else added

    def finish():
        for ip in range(ni // 2):
            for jp in range(njp):
                def halves(tile):
                    return pair_up(tile[:, :T], tile[:, T:])

                d = []
                for ii in range(2):
                    i = 2 * ip + ii
                    d.append(halves(jnp.stack(
                        [direct[h ^ labels_i[i], i * V:(i + 1) * V, 2 * V * jp:2 * V * (jp + 1)] for h in range(H)])))
                for jj in range(2):
                    j = 2 * jp + jj
                    if j >= nj:
                        continue
                    c = halves(jnp.stack(
                        [crossed[h ^ labels_j[j], j * V:(j + 1) * V, 2 * V * ip:2 * V * (ip + 1)] for h in range(H)]))
                    for ii in range(2):
                        i = 2 * ip + ii
                        out_ref[i // rows, i % rows, j] = (d[ii][jj] - c[ii]).reshape(H, V * V).astype(BF16)

    return add, finish


def scatter_kernel(npi, part_ref, out_ref, near, sums, far, near_send, near_recv, far_send, far_recv):
    p = lax.axis_index("pi")
    q = lax.axis_index("pj")
    core = p % 2
    chip = p // 2
    chips = npi // 2
    mate = chip * 2 + 1 - core
    barrier = pltpu.get_barrier_semaphore()
    pl.semaphore_signal(barrier, inc=1, device_id=(mate, q), device_id_type=MESH)
    for step in range(1, chips):
        pl.semaphore_signal(barrier, inc=1, device_id=((chip + step) % chips * 2 + core, q), device_id_type=MESH)
    pl.semaphore_wait(barrier, chips)

    def to_mate(step):
        target = (chip + step) % chips
        return pltpu.make_async_remote_copy(
            src_ref=part_ref.at[target * 2 + 1 - core], dst_ref=near.at[step], send_sem=near_send.at[step],
            recv_sem=near_recv.at[step], device_id=(mate, q), device_id_type=MESH)

    def to_chip(step):
        return pltpu.make_async_remote_copy(
            src_ref=sums.at[step], dst_ref=far.at[step], send_sem=far_send.at[step],
            recv_sem=far_recv.at[step], device_id=((chip + step) % chips * 2 + core, q), device_id_type=MESH)

    order = [*range(1, chips), 0]
    for step in order:
        to_mate(step).start()
    for step in order:
        to_mate(step).wait_recv()
        if step:
            @pl.loop(0, out_ref.shape[0])
            def _(i):
                sums[step, i] = (part_ref[(chip + step) % chips * 2 + core, i].astype(F32)
                                 + near[step, i].astype(F32)).astype(BF16)
            to_chip(step).start()
    for step in range(1, chips):
        to_chip(step).wait_recv()

    @pl.loop(0, out_ref.shape[0])
    def _(i):
        total = part_ref[p, i].astype(F32) + near[0, i].astype(F32)
        for step in range(1, chips):
            total = total + far[step, i].astype(F32)
        out_ref[i] = total.astype(BF16)

    for step in order:
        to_mate(step).wait_send()
        if step:
            to_chip(step).wait_send()


def on_device(npi, fold, amplitudes, coulomb, exchange, occ_irrep):
    rows, nka = amplitudes.shape[:2]
    nk, nj = coulomb.shape[:2]
    nkp, njp = (nk + 1) // 2, (nj + 1) // 2
    per = 3 if nka % 3 == 0 else nka
    chunks = rows * (nka // per)
    early = max(1, chunks - chunks // 2)
    sent = amplitudes.reshape((chunks, per) + amplitudes.shape[2:])
    vmem = pl.BlockSpec(memory_space=pltpu.VMEM)
    hbm = pl.BlockSpec(memory_space=pl.ANY)
    smem = pl.BlockSpec(memory_space=pltpu.SMEM)
    dma = pltpu.SemaphoreType.DMA
    limit = 60 * 2**20
    assert fold == 1 or nka % 2 == 0
    held = [
        pltpu.VMEM((npi,) + sent.shape, BF16),
        pltpu.VMEM((2, 2) + coulomb.shape[1:], BF16),
        pltpu.VMEM((2, 2) + coulomb.shape[1:], BF16),
        dma((2,)), dma((2,)), dma(()), dma((chunks,)),
        dma((npi, chunks)), dma((npi, chunks)), dma((npi, chunks)),
        dma((npi, chunks)), dma((npi, chunks)),
        dma((npi, fold, chunks)), dma((npi, fold, chunks)),
        pltpu.VMEM((2, early) + sent.shape[1:], BF16),
        dma((2, early)), dma((2, early)), dma((2, early)), dma((npi, early)), dma((2, early)), dma((early,)),
    ]
    shared = [
        ((npi, fold) + sent.shape, BF16),
        ((2 * nkp, H, V, 2 * V * njp), BF16),
        ((2 * njp, H, nkp, V, 2 * V), BF16),
    ]
    span = min(npi, 8 // rows)
    ni = span * rows
    half = (nka + 1) // 2
    worked = [
        pltpu.VMEM((ni // 2, H, 2 * half, V, 2 * V), BF16),
        pltpu.VMEM((ni, H, half, V, 2 * V), BF16),
        pltpu.VMEM((ni, H, half, V, 2 * V), BF16),
        pltpu.VMEM((H, ni * V, 2 * V * njp), F32),
        pltpu.VMEM((H, nj * V, ni * V), F32),
        pltpu.VMEM((ni * V, 2 * half * V), BF16),
        pltpu.VMEM((2 * half * V, 2 * V * njp), BF16),
        pltpu.VMEM((nj * V, 2 * half * V), BF16),
        pltpu.VMEM((2 * half * V, ni * V), BF16),
    ]
    reach = pltpu.CompilerParams(collective_id=0, has_side_effects=True, vmem_limit_bytes=limit)
    if span == npi:
        parts = pl.pallas_call(
            functools.partial(fused_kernel, npi, fold, chunks, nk, nj, rows, nka),
            out_shape=jax.ShapeDtypeStruct((npi, rows, nj) + amplitudes.shape[2:], BF16),
            in_specs=[smem, hbm, hbm, hbm],
            out_specs=vmem,
            scratch_shapes=[pltpu.VMEM(*one) for one in shared] + held + worked,
            compiler_params=reach,
        )(occ_irrep, sent, coulomb, exchange)
    else:
        gathered, ls, lt = pl.pallas_call(
            functools.partial(gather_kernel, npi, fold, chunks, nk, nj),
            out_shape=[jax.ShapeDtypeStruct(*one) for one in shared],
            in_specs=[hbm, hbm, hbm],
            out_specs=[vmem, vmem, vmem],
            scratch_shapes=held,
            compiler_params=reach,
        )(sent, coulomb, exchange)
        parts = jnp.concatenate([
            pl.pallas_call(
                functools.partial(contract_kernel, span, first * rows, fold, rows, nka, nj),
                out_shape=jax.ShapeDtypeStruct((span, rows, nj) + amplitudes.shape[2:], BF16),
                in_specs=[smem, vmem, vmem, vmem],
                out_specs=vmem,
                scratch_shapes=worked,
                compiler_params=pltpu.CompilerParams(vmem_limit_bytes=limit),
            )(occ_irrep, gathered[first:first + span], ls, lt)
            for first in range(0, npi, span)
        ])
    piece = (rows, nj) + amplitudes.shape[2:]
    chips = npi // 2
    return pl.pallas_call(
        functools.partial(scatter_kernel, npi),
        out_shape=jax.ShapeDtypeStruct(piece, BF16),
        in_specs=[vmem],
        out_specs=vmem,
        scratch_shapes=[
            pltpu.VMEM((chips,) + piece, BF16),
            pltpu.VMEM((chips,) + piece, BF16),
            pltpu.VMEM((chips,) + piece, BF16),
            dma((chips,)), dma((chips,)), dma((chips,)), dma((chips,)),
        ],
        compiler_params=pltpu.CompilerParams(collective_id=1, has_side_effects=True, vmem_limit_bytes=limit),
    )(parts)


def solution(mesh):
    npi, npj = mesh.shape["pi"], mesh.shape["pj"]
    placed = (P("pi", "pj", None, None), P("pi", "pj", None, None), P("pi", "pj", None, None), P())
    return jax.shard_map(
        functools.partial(on_device, npi, npj // npi), mesh=mesh, in_specs=placed,
        out_specs=P("pi", "pj", None, None), check_vma=False
    )
```

```python
import functools

import jax
import jax.numpy as jnp
from jax import lax
from jax.experimental import pallas as pl
from jax.experimental.pallas import tpu as pltpu
from jax.sharding import PartitionSpec as P

V = 64
H = 8
T = V // 2
MESH = pl.DeviceIdType.MESH
F32 = jnp.float32
BF16 = jnp.bfloat16
NT = (((1,), (1,)), ((), ()))


def even_odd_pair():
    row = lax.broadcasted_iota(jnp.int32, (2 * V, 2 * V), 0)
    col = lax.broadcasted_iota(jnp.int32, (2 * V, 2 * V), 1)
    inside = row % V
    source = (row // V) * V + 2 * (inside % T) + inside // T
    return (col == source).astype(F32).astype(BF16)


def low_half(shape):
    return lax.broadcasted_iota(jnp.int32, shape, len(shape) - 1) < V


def pair_up(first, second):
    low = low_half(first.shape)
    axis = first.ndim - 1
    return (
        jnp.where(low, first, pltpu.roll(second, V, axis)),
        jnp.where(low, pltpu.roll(first, V, axis), second),
    )


def split_rows(row):
    return row.reshape(H, T, 2 * V)


def stack(first, second):
    even, odd = pair_up(first, second)
    return jnp.concatenate([even, odd], axis=1).astype(BF16)


def ladder_part(kp, nk, nj, c_slot, x_slot, ls_ref, lt_ref):
    perm = even_odd_pair()

    def ladder(kk, j):
        return split_rows(2.0 * c_slot[kk, j].astype(F32) - x_slot[kk, j].astype(F32))

    for jp in range((nj + 1) // 2):
        tiles = []
        for kk in range(2):
            k = 2 * kp + kk
            if k >= nk:
                tile = jnp.zeros((H, V, 2 * V), BF16)
                ls_ref[k, :, :, 2 * V * jp:2 * V * (jp + 1)] = tile
                tiles.append(tile)
                continue
            first = ladder(kk, 2 * jp)
            second = ladder(kk, 2 * jp + 1) if 2 * jp + 1 < nj else jnp.zeros_like(first)
            tile = stack(first, second)
            ls_ref[k, :, :, 2 * V * jp:2 * V * (jp + 1)] = tile
            tiles.append(tile)
        for h in range(H):
            both = jnp.concatenate([tiles[0][h], tiles[1][h]], axis=0)
            turned = lax.dot_general(perm, both, NT, preferred_element_type=F32).astype(BF16)
            lt_ref[2 * jp, h, kp] = turned[:V]
            lt_ref[2 * jp + 1, h, kp] = turned[V:]


def gather(npi, fold, chunks, nk, nj, use, amp_ref, c_hbm, x_hbm, all_ref, ls_ref, lt_ref,
                  col, c_ref, x_ref, c_sem, x_sem, own_sem, local_sem, col_recv, up_send, down_send,
                  x_recv, x_send, y_recv, y_send,
           swapped, swap_send, swap_recv, pass_send, side_recv, side_send, side_keep):
    p = lax.axis_index("pi")
    q = lax.axis_index("pj")
    z = q // fold
    y = q % fold
    barrier = pltpu.get_barrier_semaphore()
    up = (p, q + fold)
    down = (p, q - fold)

    @pl.when(z + 1 < npi)
    def _():
        pl.semaphore_signal(barrier, inc=1, device_id=up, device_id_type=MESH)

    @pl.when(z > 0)
    def _():
        pl.semaphore_signal(barrier, inc=1, device_id=down, device_id_type=MESH)

    for step in range(1, npi):
        pl.semaphore_signal(barrier, inc=1, device_id=((p + step) % npi, q), device_id_type=MESH)
    for step in range(1, fold):
        pl.semaphore_signal(barrier, inc=1, device_id=(p, z * fold + (y + step) % fold), device_id_type=MESH)

    nkp = (nk + 1) // 2

    def loads(kp):
        slot, count = kp % 2, min(2, nk - 2 * kp)
        return (
            pltpu.make_async_copy(c_hbm.at[pl.ds(2 * kp, count)], c_ref.at[slot, pl.ds(0, count)], c_sem.at[slot]),
            pltpu.make_async_copy(x_hbm.at[pl.ds(2 * kp, count)], x_ref.at[slot, pl.ds(0, count)], x_sem.at[slot]),
        )

    own = pltpu.make_async_copy(amp_ref, col.at[z], own_sem)
    own.start()
    for kp in range(min(2, nkp)):
        for load in loads(kp):
            load.start()

    at_end = (z == 0) | (z == npi - 1)

    @pl.when(at_end)
    def _():
        pl.semaphore_wait(barrier, npi + fold - 1)

    @pl.when(jnp.logical_not(at_end))
    def _():
        pl.semaphore_wait(barrier, npi + fold)

    own.wait()

    def send_up(piece, ch):
        return pltpu.make_async_remote_copy(
            src_ref=col.at[piece, ch], dst_ref=col.at[piece, ch], send_sem=up_send.at[piece, ch],
            recv_sem=col_recv.at[piece, ch], device_id=up, device_id_type=MESH)

    def send_down(piece, ch):
        return pltpu.make_async_remote_copy(
            src_ref=col.at[piece, ch], dst_ref=col.at[piece, ch], send_sem=down_send.at[piece, ch],
            recv_sem=col_recv.at[piece, ch], device_id=down, device_id_type=MESH)

    def send_x(piece, ch):
        return pltpu.make_async_remote_copy(
            src_ref=col.at[piece, ch], dst_ref=all_ref.at[p, y, ch], send_sem=x_send.at[piece, ch],
            recv_sem=x_recv.at[p, ch], device_id=(piece, q), device_id_type=MESH)

    def keep(ch):
        return pltpu.make_async_copy(col.at[p, ch], all_ref.at[p, y, ch], local_sem.at[ch])

    def send_y(source, ch, step):
        return pltpu.make_async_remote_copy(
            src_ref=all_ref.at[source, y, ch], dst_ref=all_ref.at[source, y, ch],
            send_sem=y_send.at[source, step, ch], recv_sem=y_recv.at[source, y, ch],
            device_id=(p, z * fold + (y + step) % fold), device_id_type=MESH)

    early = list(range(chunks // 2, chunks)) if fold == 2 else []
    ends = (0, npi - 1)
    inner = (p > 0) & (p < npi - 1)
    across = (p, z * fold + (y + 1) % fold)

    def swap(end, ch):
        return pltpu.make_async_remote_copy(
            src_ref=col.at[ends[end], ch], dst_ref=swapped.at[end, early.index(ch)],
            send_sem=swap_send.at[end, early.index(ch)], recv_sem=swap_recv.at[end, early.index(ch)],
            device_id=across, device_id_type=MESH)

    def pass_on(end, ch):
        at = early.index(ch)
        return pltpu.make_async_remote_copy(
            src_ref=swapped.at[end, at], dst_ref=swapped.at[end, at], send_sem=pass_send.at[end, at],
            recv_sem=swap_recv.at[end, at], device_id=down if end else up, device_id_type=MESH)

    def send_side(end, ch):
        at = early.index(ch)
        return pltpu.make_async_remote_copy(
            src_ref=swapped.at[end, at], dst_ref=all_ref.at[p, (y + 1) % fold, ch], send_sem=side_send.at[end, at],
            recv_sem=side_recv.at[p, at], device_id=(ends[end], q), device_id_type=MESH)

    def side_from(source, ch):
        at = early.index(ch)
        return pltpu.make_async_remote_copy(
            src_ref=swapped.at[0, at], dst_ref=all_ref.at[source, (y + 1) % fold, ch], send_sem=side_send.at[0, at],
            recv_sem=side_recv.at[source, at], device_id=(source, q), device_id_type=MESH)

    def keep_side(end, ch):
        at = early.index(ch)
        return pltpu.make_async_copy(swapped.at[end, at], all_ref.at[p, (y + 1) % fold, ch], side_keep.at[at])

    def passes(end):
        return z > 0 if end else z + 1 < npi

    def place_side(end, ch):
        swap(end, ch).wait_recv()

        @pl.when(passes(end))
        def _():
            pass_on(end, ch).start()

        @pl.when(p != ends[end])
        def _():
            send_side(end, ch).start()

        @pl.when(p == ends[end])
        def _():
            keep_side(end, ch).start()

    def send_own_y(ch, step):
        return pltpu.make_async_remote_copy(
            src_ref=col.at[p, ch], dst_ref=all_ref.at[p, y, ch],
            send_sem=y_send.at[p, step, ch], recv_sem=y_recv.at[p, y, ch],
            device_id=(p, z * fold + (y + step) % fold), device_id_type=MESH)

    def place(piece, ch):
        @pl.when(piece != p)
        def _():
            send_x(piece, ch).start()

        @pl.when(piece == p)
        def _():
            keep(ch).start()

        @pl.when((piece == p) & (inner | (ch not in early)))
        def _():
            for step in range(1, fold):
                send_own_y(ch, step).start()

    away = jnp.where(z > p, z - p, p - z)
    lag = 2

    def forward_y(event):
        if fold > 1 and 0 <= event < npi * chunks:
            ch = event % chunks

            @pl.when(away == event // chunks)
            def _():
                for shift in range(1, npi):
                    source = (p + shift) % npi
                    send_x_from(source, ch).wait_recv()

                    @pl.when(inner | (ch not in early))
                    def _():
                        for step in range(1, fold):
                            send_y(source, ch, step).start()

    def send_x_from(source, ch):
        return pltpu.make_async_remote_copy(
            src_ref=col.at[0, ch], dst_ref=all_ref.at[source, y, ch], send_sem=x_send.at[0, ch],
            recv_sem=x_recv.at[source, ch], device_id=(source, q), device_id_type=MESH)

    for ch in range(chunks):
        @pl.when(z + 1 < npi)
        def _():
            send_up(z, ch).start()

        @pl.when(z > 0)
        def _():
            send_down(z, ch).start()

        if ch in early:
            for end in range(2):
                @pl.when(z == ends[end])
                def _():
                    swap(end, ch).start()

        place(z, ch)

    parts = list(range(nkp))

    def some_ladder():
        if parts:
            kp = parts.pop(0)
            for load in loads(kp):
                load.wait()
            ladder_part(kp, nk, nj, c_ref.at[kp % 2], x_ref.at[kp % 2], ls_ref, lt_ref)
            if kp + 2 < nkp:
                for load in loads(kp + 2):
                    load.start()

    some_ladder()
    for event in range(chunks, npi * chunks):
        far, ch = event // chunks, event % chunks
        below = z - far
        above = z + far

        @pl.when(below >= 0)
        def _():
            send_up(below, ch).wait_recv()

            @pl.when(z + 1 < npi)
            def _():
                send_up(below, ch).start()

            place(below, ch)

        @pl.when(above < npi)
        def _():
            send_down(above, ch).wait_recv()

            @pl.when(z > 0)
            def _():
                send_down(above, ch).start()

            place(above, ch)

        if ch in early:
            @pl.when(below == 0)
            def _():
                place_side(0, ch)

            @pl.when(above == npi - 1)
            def _():
                place_side(1, ch)

        if far == 1 and chunks - 1 - ch in early:
            for end in range(2):
                @pl.when(z == ends[end])
                def _():
                    place_side(end, early[ch])

        if event == chunks:
            for first in range(chunks - lag):
                forward_y(first)
        forward_y(event - lag)
        some_ladder()
    while parts:
        some_ladder()
    for late in range(npi * chunks - lag, npi * chunks):
        forward_y(late)

    for ch in range(chunks):
        keep(ch).wait()
        if fold == 1:
            for shift in range(1, npi):
                send_x_from((p + shift) % npi, ch).wait_recv()
    use(0)
    for half in range(1, fold):
        other = (y + half) % fold
        for ch in range(chunks):
            @pl.when(inner | (ch not in early))
            def _():
                for source in range(npi):
                    pltpu.make_async_remote_copy(
                        src_ref=all_ref.at[source, other, ch], dst_ref=all_ref.at[source, other, ch],
                        send_sem=y_send.at[source, half, ch], recv_sem=y_recv.at[source, other, ch],
                        device_id=(p, z * fold + other), device_id_type=MESH).wait_recv()

            if ch in early:
                @pl.when(jnp.logical_not(inner))
                def _():
                    for shift in range(1, npi):
                        side_from((p + shift) % npi, ch).wait_recv()
                    keep_side(0, ch).wait()

        use(half)

    for ch in range(chunks):
        @pl.when(inner | (ch not in early))
        def _():
            for source in range(npi):
                for step in range(1, fold):
                    send_y(source, ch, step).wait_send()

        if ch in early:
            for end in range(2):
                @pl.when(z == ends[end])
                def _():
                    swap(end, ch).wait_send()

                @pl.when(passes(end))
                def _():
                    pass_on(end, ch).wait_send()

                @pl.when(p != ends[end])
                def _():
                    send_side(end, ch).wait_send()

        for piece in range(npi):
            @pl.when((piece <= z) & (z + 1 < npi))
            def _():
                send_up(piece, ch).wait_send()

            @pl.when((piece >= z) & (z > 0))
            def _():
                send_down(piece, ch).wait_send()

            @pl.when(piece != p)
            def _():
                send_x(piece, ch).wait_send()


def gather_kernel(npi, fold, chunks, nk, nj, *refs):
    gather(npi, fold, chunks, nk, nj, lambda half: None, *refs)


def fused_kernel(npi, fold, chunks, nk, nj, rows, nka, label_ref, amp_ref, c_hbm, x_hbm, out_ref,
                 all_ref, ls_ref, lt_ref, *scratch):
    held = len(scratch) - 9
    steps = contraction(npi, 0, fold, rows, nka, nj, label_ref, all_ref, ls_ref, lt_ref, out_ref, *scratch[held:])

    def use(half):
        steps[0](half)
        if half == fold - 1:
            steps[1]()

    gather(npi, fold, chunks, nk, nj, use, amp_ref, c_hbm, x_hbm, all_ref, ls_ref, lt_ref, *scratch[:held])


def contract_kernel(npi, first_i, fold, *rest):
    steps = contraction(npi, first_i, fold, *rest)
    for half in range(fold):
        steps[0](half)
    steps[1]()


def contraction(npi, first_i, fold, rows, nka, nj, label_ref, all_ref, ls_ref, lt_ref, out_ref,
                as_ref, qs_ref, qt_ref, direct, crossed, left, right, cross_left, cross_right):
    p = lax.axis_index("pi")
    q = lax.axis_index("pj")
    y = q % fold
    ni = npi * rows
    nkp = (nka + 1) // 2
    njp = (nj + 1) // 2
    ck = all_ref.shape[3]
    nck = nka // ck
    labels_i = [label_ref[first_i + i] for i in range(ni)]
    labels_j = [label_ref[q * nj + j] for j in range(nj)]

    def add(half):
        part = (y + half) % fold
        perm = even_odd_pair()
        low = low_half((V, 2 * V))
        labels_k = [label_ref[(p * fold + part) * nka + min(k, nka - 1)] for k in range(2 * nkp)]

        @pl.loop(0, ni // 2)
        def _(ip):
            for kp in range(nkp):
                def block(ii, kk):
                    i = 2 * ip + ii
                    k = 2 * kp + kk
                    if k >= nka:
                        return jnp.zeros((H, T, 2 * V), F32)
                    chunk = (i % rows) * nck + k // ck
                    return split_rows(all_ref[i // rows, part, chunk, k % ck].astype(F32))

                b00, b01, b10, b11 = block(0, 0), block(0, 1), block(1, 0), block(1, 1)
                side0 = stack(b00, b10)
                side1 = stack(b01, b11)
                as_ref[ip, :, 2 * kp] = side0
                as_ref[ip, :, 2 * kp + 1] = side1
                along0 = stack(b00, b01)
                along1 = stack(b10, b11)
                for h in range(H):
                    both = jnp.concatenate([side0[h], side1[h]], axis=0)
                    turned = lax.dot_general(perm, both, NT, preferred_element_type=F32).astype(BF16)
                    qt_ref[2 * ip, h, kp] = turned[:V]
                    qt_ref[2 * ip + 1, h, kp] = turned[V:]
                    both = jnp.concatenate([along0[h], along1[h]], axis=0)
                    moved = lax.dot_general(both, perm, NT, preferred_element_type=F32).astype(BF16)
                    qs_ref[2 * ip, h, kp] = moved[:V]
                    qs_ref[2 * ip + 1, h, kp] = moved[V:]

        @pl.loop(0, H)
        def _(u):
            at = [u ^ label for label in labels_k]
            for k in range(2 * nkp):
                right[k * V:(k + 1) * V] = ls_ref[part * 2 * nkp + k, at[k]]
                for ip in range(ni // 2):
                    cross_right[k * V:(k + 1) * V, 2 * V * ip:2 * V * (ip + 1)] = as_ref[ip, at[k], k]
            for kp in range(nkp):
                lanes = slice(2 * V * kp, 2 * V * (kp + 1))
                g0, g1 = at[2 * kp], at[2 * kp + 1]
                for i in range(ni):
                    turned = jnp.where(low, qt_ref[i, g0, kp].astype(F32), qt_ref[i, g1, kp].astype(F32))
                    left[i * V:(i + 1) * V, lanes] = (
                        2.0 * qs_ref[i, u ^ labels_i[i], kp].astype(F32) - turned).astype(BF16)
                for j in range(nj):
                    from_k = part * nkp + kp
                    cross_left[j * V:(j + 1) * V, lanes] = jnp.where(
                        low, lt_ref[j, g0, from_k].astype(F32), lt_ref[j, g1, from_k].astype(F32)).astype(BF16)
            added = jnp.dot(left[...], right[...], preferred_element_type=F32)
            direct[u] = direct[u] + added if half else added
            added = jnp.dot(cross_left[...], cross_right[...], preferred_element_type=F32)
            crossed[u] = crossed[u] + added if half else added

    def finish():
        for ip in range(ni // 2):
            for jp in range(njp):
                def halves(tile):
                    return pair_up(tile[:, :T], tile[:, T:])

                d = []
                for ii in range(2):
                    i = 2 * ip + ii
                    d.append(halves(jnp.stack(
                        [direct[h ^ labels_i[i], i * V:(i + 1) * V, 2 * V * jp:2 * V * (jp + 1)] for h in range(H)])))
                for jj in range(2):
                    j = 2 * jp + jj
                    if j >= nj:
                        continue
                    c = halves(jnp.stack(
                        [crossed[h ^ labels_j[j], j * V:(j + 1) * V, 2 * V * ip:2 * V * (ip + 1)] for h in range(H)]))
                    for ii in range(2):
                        i = 2 * ip + ii
                        out_ref[i // rows, i % rows, j] = (d[ii][jj] - c[ii]).reshape(H, V * V).astype(BF16)

    return add, finish


def scatter_kernel(npi, part_ref, out_ref, near, sums, far, near_send, near_recv, far_send, far_recv):
    p = lax.axis_index("pi")
    q = lax.axis_index("pj")
    core = p % 2
    chip = p // 2
    chips = npi // 2
    mate = chip * 2 + 1 - core
    barrier = pltpu.get_barrier_semaphore()
    pl.semaphore_signal(barrier, inc=1, device_id=(mate, q), device_id_type=MESH)
    for step in range(1, chips):
        pl.semaphore_signal(barrier, inc=1, device_id=((chip + step) % chips * 2 + core, q), device_id_type=MESH)
    pl.semaphore_wait(barrier, chips)

    rows = out_ref.shape[0]

    def to_mate(step, i):
        target = (chip + step) % chips
        return pltpu.make_async_remote_copy(
            src_ref=part_ref.at[target * 2 + 1 - core, i], dst_ref=near.at[step, i], send_sem=near_send.at[step, i],
            recv_sem=near_recv.at[step, i], device_id=(mate, q), device_id_type=MESH)

    def to_chip(step, i):
        return pltpu.make_async_remote_copy(
            src_ref=sums.at[step, i], dst_ref=far.at[step, i], send_sem=far_send.at[step, i],
            recv_sem=far_recv.at[step, i], device_id=((chip + step) % chips * 2 + core, q), device_id_type=MESH)

    order = [(step, i) for step in [*range(1, chips), 0] for i in range(rows)]
    for step, i in order:
        to_mate(step, i).start()
    for step, i in order:
        to_mate(step, i).wait_recv()
        if step:
            sums[step, i] = (part_ref[(chip + step) % chips * 2 + core, i].astype(F32)
                             + near[step, i].astype(F32)).astype(BF16)
            to_chip(step, i).start()
    for i in range(rows):
        for step in range(1, chips):
            to_chip(step, i).wait_recv()
        total = part_ref[p, i].astype(F32) + near[0, i].astype(F32)
        for step in range(1, chips):
            total = total + far[step, i].astype(F32)
        out_ref[i] = total.astype(BF16)

    for step, i in order:
        to_mate(step, i).wait_send()
        if step:
            to_chip(step, i).wait_send()


def on_device(npi, fold, amplitudes, coulomb, exchange, occ_irrep):
    rows, nka = amplitudes.shape[:2]
    nk, nj = coulomb.shape[:2]
    nkp, njp = (nk + 1) // 2, (nj + 1) // 2
    per = 3 if nka % 3 == 0 else nka
    chunks = rows * (nka // per)
    early = max(1, chunks - chunks // 2)
    sent = amplitudes.reshape((chunks, per) + amplitudes.shape[2:])
    vmem = pl.BlockSpec(memory_space=pltpu.VMEM)
    hbm = pl.BlockSpec(memory_space=pl.ANY)
    smem = pl.BlockSpec(memory_space=pltpu.SMEM)
    dma = pltpu.SemaphoreType.DMA
    limit = 60 * 2**20
    assert fold == 1 or nka % 2 == 0
    held = [
        pltpu.VMEM((npi,) + sent.shape, BF16),
        pltpu.VMEM((2, 2) + coulomb.shape[1:], BF16),
        pltpu.VMEM((2, 2) + coulomb.shape[1:], BF16),
        dma((2,)), dma((2,)), dma(()), dma((chunks,)),
        dma((npi, chunks)), dma((npi, chunks)), dma((npi, chunks)),
        dma((npi, chunks)), dma((npi, chunks)),
        dma((npi, fold, chunks)), dma((npi, fold, chunks)),
        pltpu.VMEM((2, early) + sent.shape[1:], BF16),
        dma((2, early)), dma((2, early)), dma((2, early)), dma((npi, early)), dma((2, early)), dma((early,)),
    ]
    shared = [
        ((npi, fold) + sent.shape, BF16),
        ((2 * nkp, H, V, 2 * V * njp), BF16),
        ((2 * njp, H, nkp, V, 2 * V), BF16),
    ]
    span = min(npi, 8 // rows)
    ni = span * rows
    half = (nka + 1) // 2
    worked = [
        pltpu.VMEM((ni // 2, H, 2 * half, V, 2 * V), BF16),
        pltpu.VMEM((ni, H, half, V, 2 * V), BF16),
        pltpu.VMEM((ni, H, half, V, 2 * V), BF16),
        pltpu.VMEM((H, ni * V, 2 * V * njp), F32),
        pltpu.VMEM((H, nj * V, ni * V), F32),
        pltpu.VMEM((ni * V, 2 * half * V), BF16),
        pltpu.VMEM((2 * half * V, 2 * V * njp), BF16),
        pltpu.VMEM((nj * V, 2 * half * V), BF16),
        pltpu.VMEM((2 * half * V, ni * V), BF16),
    ]
    reach = pltpu.CompilerParams(collective_id=0, has_side_effects=True, vmem_limit_bytes=limit)
    if span == npi:
        parts = pl.pallas_call(
            functools.partial(fused_kernel, npi, fold, chunks, nk, nj, rows, nka),
            out_shape=jax.ShapeDtypeStruct((npi, rows, nj) + amplitudes.shape[2:], BF16),
            in_specs=[smem, hbm, hbm, hbm],
            out_specs=vmem,
            scratch_shapes=[pltpu.VMEM(*one) for one in shared] + held + worked,
            compiler_params=reach,
        )(occ_irrep, sent, coulomb, exchange)
    else:
        gathered, ls, lt = pl.pallas_call(
            functools.partial(gather_kernel, npi, fold, chunks, nk, nj),
            out_shape=[jax.ShapeDtypeStruct(*one) for one in shared],
            in_specs=[hbm, hbm, hbm],
            out_specs=[vmem, vmem, vmem],
            scratch_shapes=held,
            compiler_params=reach,
        )(sent, coulomb, exchange)
        parts = jnp.concatenate([
            pl.pallas_call(
                functools.partial(contract_kernel, span, first * rows, fold, rows, nka, nj),
                out_shape=jax.ShapeDtypeStruct((span, rows, nj) + amplitudes.shape[2:], BF16),
                in_specs=[smem, vmem, vmem, vmem],
                out_specs=vmem,
                scratch_shapes=worked,
                compiler_params=pltpu.CompilerParams(vmem_limit_bytes=limit),
            )(occ_irrep, gathered[first:first + span], ls, lt)
            for first in range(0, npi, span)
        ])
    piece = (rows, nj) + amplitudes.shape[2:]
    chips = npi // 2
    return pl.pallas_call(
        functools.partial(scatter_kernel, npi),
        out_shape=jax.ShapeDtypeStruct(piece, BF16),
        in_specs=[vmem],
        out_specs=vmem,
        scratch_shapes=[
            pltpu.VMEM((chips,) + piece, BF16),
            pltpu.VMEM((chips,) + piece, BF16),
            pltpu.VMEM((chips,) + piece, BF16),
            dma((chips, rows)), dma((chips, rows)), dma((chips, rows)), dma((chips, rows)),
        ],
        compiler_params=pltpu.CompilerParams(collective_id=1, has_side_effects=True, vmem_limit_bytes=limit),
    )(parts)


def solution(mesh):
    npi, npj = mesh.shape["pi"], mesh.shape["pj"]
    placed = (P("pi", "pj", None, None), P("pi", "pj", None, None), P("pi", "pj", None, None), P())
    return jax.shard_map(
        functools.partial(on_device, npi, npj // npi), mesh=mesh, in_specs=placed,
        out_specs=P("pi", "pj", None, None), check_vma=False
    )
```
